32 devices in a mesh: view: 2 (over x), band: 4 (over z), batch: 4 (over y, core).
Axes of the slice: x: 2, y: 2, z: 4, core: 2. Of those that a mesh axis runs over, the one named last changes fastest.
Arguments:
- images: bfloat16 [8, 32, 16, 768], P(('batch', 'view'), 'band'), parts along dimension 0, may hold values from -6 to 6
- frame_gain: float32 [768], replicated, may hold values from 0.5 to 2.5
- frame_qkv: bfloat16 [768, 1536], replicated, may hold values from -0.3 to 0.3
- frame_out: bfloat16 [512, 768], replicated, may hold values from -0.25 to 0.25
- row1_gain: float32 [768], replicated, may hold values from 0.5 to 2.5
- row1_qkv: bfloat16 [768, 1536], P('band'), may hold values from -0.3 to 0.3
- row1_out: bfloat16 [512, 768], P(None, 'band'), may hold values from -0.25 to 0.25
- row2_gain: float32 [768], replicated, may hold values from 0.5 to 2.5
- row2_qkv: bfloat16 [768, 1536], P('band'), may hold values from -0.3 to 0.3
- row2_out: bfloat16 [512, 768], P(None, 'band'), may hold values from -0.25 to 0.25
Outputs:
- refined: bfloat16 [8, 32, 16, 768], P(('batch', 'view'), 'band'), parts along dimension 0
The draws below stay inside these ranges and needn't reach their ends.
There are 4 independent parts, one for each index of `batch`. The reference program is written for one: setup_inputs(seed, part) draws one part's arguments, and reference() takes and returns one part's arrays. A program takes and returns all parts, laid end to end along the dimension named above; an argument that names none is the same for every part. Nothing has to cross between parts.
All inputs are finite; a program needn't handle non-finite values.
Results may differ from the reference program's by a relative error of at most 0.02.
Values may be sent and summed in bfloat16 or wider, within the bound.
A program may use at most 64 MiB of HBM per device.

```python
import jax
import jax.numpy as jnp
from jax import lax

D = 768
HEAD_DIM = 64
HEADS = 8
COLS = 16
VIEWS = 2
HEIGHT = 32
E = 512


def gain_values(key):
    return jax.random.uniform(key, (D,), minval=0.5, maxval=1.5)


def projection_values(key):
    inner = HEADS * HEAD_DIM
    query_key, key_key, value_key = jax.random.split(key, 3)
    spread = 1.4 * D ** (-0.5)
    queries = jax.random.normal(query_key, (D, inner)) * spread
    fresh = jax.random.normal(key_key, (D, inner)) * spread
    keys = fresh
    values = jax.random.normal(value_key, (D, inner)) * D ** (-0.5)
    return jnp.clip(jnp.concatenate([queries, keys, values], axis=1), -0.29, 0.29).astype(jnp.bfloat16)


def draw_images(key, part):
    key = jax.random.fold_in(key, 31)
    shape = (VIEWS, HEIGHT, COLS, D)
    base_key = jax.random.fold_in(key, 0)
    values = jax.random.normal(base_key, shape)
    return jnp.clip(values, -6.0, 6.0).astype(jnp.bfloat16)


def draw_frame_gain(key, part):
    return gain_values(jax.random.fold_in(key, 11))


def draw_row1_gain(key, part):
    return gain_values(jax.random.fold_in(key, 12))


def draw_row2_gain(key, part):
    return gain_values(jax.random.fold_in(key, 13))


def draw_frame_qkv(key, part):
    return projection_values(jax.random.fold_in(key, 21))


def draw_row1_qkv(key, part):
    return projection_values(jax.random.fold_in(key, 22))


def draw_row2_qkv(key, part):
    return projection_values(jax.random.fold_in(key, 23))


def block_levels(key, shape, shards, low, largest):
    loudness = 1.0
    for axis_at, parts in shards:
        heights = jax.random.uniform(jax.random.fold_in(jax.random.fold_in(key, 6), axis_at), (parts,), jnp.float32, low / len(shards), largest / len(shards))
        loudness = loudness * jnp.repeat(jnp.exp(heights), shape[axis_at] // parts).reshape((-1,) + (1,) * (len(shape) - 1 - axis_at))
    return loudness


def scatter_about(own_key, dims, deviation, most, cuts=(), kind=jnp.bfloat16):
    result = deviation * jax.random.normal(own_key, dims, jnp.float32)
    if cuts:
        result = result * block_levels(own_key, dims, cuts, -0.22, 0.18)
    return jnp.clip(result, -most, most).astype(kind)


def setup_inputs(seed: int = 0, part: int = 0) -> dict:
    splits = jax.random.split(jax.random.key(seed), 11)
    own_keys = jax.random.split(jax.random.fold_in(splits[10], part), 11)
    return {
        "images": draw_images(jax.random.fold_in(jax.random.fold_in(splits[10], part), 71), part),
        "frame_gain": draw_frame_gain(jax.random.fold_in(splits[10], 71), part),
        "frame_qkv": draw_frame_qkv(jax.random.fold_in(splits[10], 71), part),
        "frame_out": scatter_about(splits[3], (E, D), E ** -0.5, 0.25),
        "row1_gain": draw_row1_gain(jax.random.fold_in(splits[10], 71), part),
        "row1_qkv": draw_row1_qkv(jax.random.fold_in(splits[10], 71), part),
        "row1_out": scatter_about(splits[6], (E, D), E ** -0.5, 0.25, ((1, 4),)),
        "row2_gain": draw_row2_gain(jax.random.fold_in(splits[10], 71), part),
        "row2_qkv": draw_row2_qkv(jax.random.fold_in(splits[10], 71), part),
        "row2_out": scatter_about(splits[9], (E, D), E ** -0.5, 0.25, ((1, 4),)),
    }


def normalize(stream, gain):
    values = stream.astype(jnp.float32)
    factor = lax.rsqrt(lax.optimization_barrier(jnp.mean(values * values, axis=-1, keepdims=True)) + 1e-06)
    return (values * factor * gain).astype(jnp.bfloat16)

def attention(queries, keys, values):
    scores = jnp.einsum('qhd,khd->hqk', queries.astype(jnp.float32), keys.astype(jnp.float32)) * HEAD_DIM ** (-0.5)
    highest = lax.optimization_barrier(jnp.max(scores, axis=-1, keepdims=True))
    weights = jnp.exp(scores - highest)
    rounded = lax.optimization_barrier(weights.astype(jnp.bfloat16)).astype(jnp.float32)
    mixed = jnp.einsum('hqk,khd->qhd', rounded, values.astype(jnp.float32))
    total = jnp.transpose(lax.optimization_barrier(jnp.sum(weights, axis=-1)))
    return (mixed / total[:, :, None]).astype(jnp.bfloat16)

def project_attend(normed, qkv_weight, out_weight):
    tokens = normed.shape[0]
    inner = HEADS * HEAD_DIM
    triple = jnp.dot(normed, qkv_weight, preferred_element_type=jnp.float32).astype(jnp.bfloat16)
    triple = triple.reshape(tokens, 3, HEADS, HEAD_DIM)
    attended = attention(triple[:, 0], triple[:, 1], triple[:, 2]).reshape(tokens, inner)
    return jnp.dot(attended, out_weight, preferred_element_type=jnp.float32)

def row_layer(stream, gain, qkv_weight, out_weight):
    views, height, columns, width = stream.shape
    normed = normalize(stream, gain)
    rows_first = jnp.transpose(normed, (1, 0, 2, 3))

    def one_row(image_row):
        update = project_attend(image_row.reshape(views * columns, width), qkv_weight, out_weight)
        return update.reshape(views, columns, width)
    update = jnp.transpose(lax.map(one_row, rows_first), (1, 0, 2, 3))
    return (stream.astype(jnp.float32) + update).astype(jnp.bfloat16)

def reference(images, frame_gain, frame_qkv, frame_out, row1_gain, row1_qkv, row1_out, row2_gain, row2_qkv, row2_out):
    views, height, columns, width = images.shape
    normed = normalize(images, frame_gain)

    def one_view(frame):
        update = project_attend(frame.reshape(height * columns, width), frame_qkv, frame_out)
        return update.reshape(height, columns, width)
    update = lax.map(one_view, normed)
    stream = (images.astype(jnp.float32) + update).astype(jnp.bfloat16)
    stream = row_layer(stream, row1_gain, row1_qkv, row1_out)
    return row_layer(stream, row2_gain, row2_qkv, row2_out)
```

```python
import functools

import jax
import jax.numpy as jnp
from jax import lax
from jax.experimental import pallas as pl
from jax.experimental.pallas import tpu as pltpu
from jax.sharding import PartitionSpec as P

HEAD_DIM = 64


EPSILON = 1e-06
BLOCK_ROWS = 512


def rms_normed(stream, gain):
    values = stream.astype(jnp.float32)
    factor = lax.rsqrt(jnp.mean(values * values, axis=-1, keepdims=True) + EPSILON)
    return (values * factor * gain).astype(jnp.bfloat16)


def online_update(carry, queries, keys, values):
    running, total, accum = carry
    scores = jnp.einsum(
        "qhd,khd->hqk", queries, keys, preferred_element_type=jnp.float32
    ) * HEAD_DIM ** (-0.5)
    highest = jnp.maximum(running, jnp.max(scores, axis=-1))
    weights = jnp.exp(scores - highest[:, :, None])
    total = jnp.sum(weights, axis=-1)
    mixed = jnp.einsum(
        "hqk,khd->qhd", weights.astype(jnp.bfloat16), values, preferred_element_type=jnp.float32
    )
    accum = mixed
    return (highest, total, accum)


def unit_attention(trio):
    queries, keys, values = trio
    length, pair_width = queries.shape
    block = min(BLOCK_ROWS, length)
    keys = keys.reshape(length, 2, HEAD_DIM)
    values = values.reshape(length, 2, HEAD_DIM)
    blocks = queries.reshape(length // block, block, 2, HEAD_DIM)

    def one_block(query_block):
        scores = jnp.einsum(
            "qhd,khd->hqk", query_block, keys, preferred_element_type=jnp.float32
        ) * HEAD_DIM ** (-0.5)
        weights = jnp.exp(scores - jnp.max(scores, axis=-1, keepdims=True))
        mixed = jnp.einsum(
            "hqk,khd->qhd", weights.astype(jnp.bfloat16), values, preferred_element_type=jnp.float32
        )
        total = jnp.transpose(jnp.sum(weights, axis=-1))
        return (mixed / total[:, :, None]).astype(jnp.bfloat16).reshape(block, pair_width)

    return lax.map(one_block, blocks).reshape(length, pair_width)


def attend_units(pieces):
    queries, keys, values = pieces
    attended = lax.map(unit_attention, (queries[0], keys[0], values[0]))
    return lax.all_to_all(attended[None], "view", split_axis=2, concat_axis=0, tiled=True)


def project_parts(normed, shard):
    groups = shard.shape[1] // (2 * HEAD_DIM)
    piece = lax.all_gather(shard, "band", axis=0, tiled=True)
    count = piece.shape[0]
    return jnp.einsum(
        "rcd,dpw->rpcw",
        normed,
        piece.reshape(count, groups, 2 * HEAD_DIM),
        preferred_element_type=jnp.float32,
    )


def mix_parts(merged, shard):
    groups = merged.shape[1]
    piece = lax.all_gather(shard, "band", axis=1, tiled=True)
    count = piece.shape[1]
    return jnp.einsum(
        "rpcw,pwn->rcn",
        merged,
        piece.reshape(groups, 2 * HEAD_DIM, count),
        preferred_element_type=jnp.float32,
    )


def row_sublayer(stream, row_count, col_count, gain, project, mix):
    width = stream.shape[1]
    normed = rms_normed(stream, gain).reshape(row_count, col_count, width)
    projected = project(normed)
    groups = projected.shape[1] // 3
    views = lax.axis_size("view")

    def unit_layout(section):
        return section.astype(jnp.bfloat16).reshape(
            views, row_count * groups // views, col_count, 2 * HEAD_DIM
        )

    triple = (
        unit_layout(projected[:, :groups]),
        unit_layout(projected[:, groups : 2 * groups]),
        unit_layout(projected[:, 2 * groups :]),
    )
    returned = attend_units(
        (
            lax.all_to_all(triple[0], "view", split_axis=0, concat_axis=2, tiled=True),
            lax.all_to_all(triple[1], "view", split_axis=0, concat_axis=2, tiled=True),
            lax.all_to_all(triple[2], "view", split_axis=0, concat_axis=2, tiled=True),
        )
    )
    merged = returned.reshape(row_count, groups, col_count, 2 * HEAD_DIM)
    update = mix(merged).reshape(row_count * col_count, width)
    return (stream.astype(jnp.float32) + update).astype(jnp.bfloat16)


def attend_pair(queries, keys, values, mask):
    lane = lax.broadcasted_iota(jnp.int32, queries.shape, 1)
    sides = []
    for side in range(2):
        own = (lane >= side * HEAD_DIM) & (lane < (side + 1) * HEAD_DIM)
        scores = lax.dot_general(
            jnp.where(own, queries, jnp.zeros_like(queries)),
            keys,
            (((1,), (1,)), ((), ())),
            preferred_element_type=jnp.float32,
        ) * HEAD_DIM ** (-0.5)
        if mask is not None:
            scores = jnp.where(mask, scores, -jnp.inf)
        weights = jnp.exp(scores - jnp.max(scores, axis=-1, keepdims=True))
        total = jnp.sum(weights, axis=-1, keepdims=True)
        mixed = jnp.dot(weights.astype(jnp.bfloat16), values, preferred_element_type=jnp.float32)
        sides.append(mixed / total)
    return jnp.where(lane < HEAD_DIM, sides[0], sides[1]).astype(jnp.bfloat16)


def row_layer(stream, gain, weights, inner, mask):
    pair = 2 * HEAD_DIM
    normed = rms_normed(stream, gain)
    projected = jnp.dot(normed, weights[:, : 3 * inner], preferred_element_type=jnp.float32)
    projected = projected.astype(jnp.bfloat16)
    parts = []
    for at in range(0, inner, pair):
        parts.append(
            attend_pair(
                projected[:, at : at + pair],
                projected[:, inner + at : inner + at + pair],
                projected[:, 2 * inner + at : 2 * inner + at + pair],
                mask,
            )
        )
    attended = jnp.concatenate(parts, axis=1)
    update = lax.dot_general(
        attended,
        weights[:, 3 * inner :],
        (((1,), (1,)), ((), ())),
        preferred_element_type=jnp.float32,
    )
    return (stream.astype(jnp.float32) + update).astype(jnp.bfloat16)


def row_mask(tokens, rows, cols):
    def row_of(dim):
        at = lax.broadcasted_iota(jnp.int32, (tokens, tokens), dim)
        return lax.rem(lax.div(at, cols), rows)

    return row_of(0) == row_of(1)


def rows_kernel(inner, rows, cols, x_ref, g1_ref, w1_ref, g2_ref, w2_ref, o_ref):
    stream = x_ref[...]
    mask = row_mask(stream.shape[0], rows, cols)
    stream = row_layer(stream, g1_ref[...], w1_ref[...], inner, mask)
    o_ref[...] = row_layer(stream, g2_ref[...], w2_ref[...], inner, mask)


def gathered_weights(qkv, out):
    joined = jnp.concatenate([qkv, out.T], axis=1)
    shares = lax.axis_size("batch") * lax.axis_size("view")
    count = joined.shape[0] // shares
    index = lax.axis_index("batch") * lax.axis_size("view") + lax.axis_index("view")
    share = lax.dynamic_slice_in_dim(joined, index * count, count, axis=0)
    return lax.all_gather(share, ("band", "batch", "view"), axis=0, tiled=True)


def frame_sublayer(stream, gain, qkv, out):
    inner = out.shape[0]
    heads = inner // HEAD_DIM
    tokens = stream.shape[0]
    normed = rms_normed(stream, gain)
    queries = (
        jnp.dot(normed, qkv[:, :inner], preferred_element_type=jnp.float32)
        .astype(jnp.bfloat16)
        .reshape(tokens, heads, HEAD_DIM)
    )
    piece = lax.all_gather(normed, "band", axis=0, tiled=True)
    count = piece.shape[0]
    paired = jnp.dot(piece, qkv[:, inner:], preferred_element_type=jnp.float32).astype(jnp.bfloat16)
    _, total, accum = online_update(
        (jnp.full((heads, tokens), -1e30, jnp.float32), None, None),
        queries,
        paired[:, :inner].reshape(count, heads, HEAD_DIM),
        paired[:, inner:].reshape(count, heads, HEAD_DIM),
    )
    attended = (accum / jnp.transpose(total)[:, :, None]).astype(jnp.bfloat16)
    update = jnp.dot(attended.reshape(tokens, inner), out, preferred_element_type=jnp.float32)
    return (stream.astype(jnp.float32) + update).astype(jnp.bfloat16)


def local_swapped(
    images,
    frame_gain,
    frame_qkv,
    frame_out,
    row1_gain,
    row1_qkv,
    row1_out,
    row2_gain,
    row2_qkv,
    row2_out,
):
    _, row_count, col_count, width = images.shape
    inner = frame_out.shape[0]
    tokens = row_count * col_count
    views = lax.axis_size("view")
    first = gathered_weights(row1_qkv, row1_out)
    second = gathered_weights(row2_qkv, row2_out)
    stream = frame_sublayer(images.reshape(tokens, width), frame_gain, frame_qkv, frame_out)
    swapped = lax.all_to_all(stream, "view", split_axis=0, concat_axis=0, tiled=True)
    refined = pl.pallas_call(
        functools.partial(rows_kernel, inner, row_count // views, col_count),
        out_shape=jax.ShapeDtypeStruct((tokens, width), jnp.bfloat16),
        compiler_params=pltpu.CompilerParams(vmem_limit_bytes=48 * 1024 * 1024),
    )(swapped, row1_gain[None], first, row2_gain[None], second)
    back = lax.all_to_all(refined, "view", split_axis=0, concat_axis=0, tiled=True)
    return back.reshape(images.shape)


def local(
    images,
    frame_gain,
    frame_qkv,
    frame_out,
    row1_gain,
    row1_qkv,
    row1_out,
    row2_gain,
    row2_qkv,
    row2_out,
):
    _, row_count, col_count, width = images.shape
    inner = frame_out.shape[0]
    heads = inner // HEAD_DIM
    tokens = row_count * col_count
    stream = images.reshape(tokens, width)
    normed = rms_normed(stream, frame_gain)
    start_state = (
        jnp.full((heads, tokens), -1e30, jnp.float32),
        jnp.zeros((heads, tokens), jnp.float32),
        jnp.zeros((tokens, heads, HEAD_DIM), jnp.float32),
    )
    queries = (
        jnp.dot(normed, frame_qkv[:, :inner], preferred_element_type=jnp.float32)
        .astype(jnp.bfloat16)
        .reshape(tokens, heads, HEAD_DIM)
    )
    piece = lax.all_gather(normed, "band", axis=0, tiled=True)
    count = piece.shape[0]
    paired = jnp.dot(piece, frame_qkv[:, inner:], preferred_element_type=jnp.float32).astype(
        jnp.bfloat16
    )
    result = online_update(
        start_state,
        queries,
        paired[:, :inner].reshape(count, heads, HEAD_DIM),
        paired[:, inner:].reshape(count, heads, HEAD_DIM),
    )
    _, total, accum = result
    attended = (
        (accum / jnp.transpose(total)[:, :, None]).astype(jnp.bfloat16).reshape(tokens, inner)
    )
    update = jnp.dot(attended, frame_out, preferred_element_type=jnp.float32)
    stream = (stream.astype(jnp.float32) + update).astype(jnp.bfloat16)
    stream = row_sublayer(
        stream,
        row_count,
        col_count,
        row1_gain,
        lambda normed_rows: project_parts(normed_rows, row1_qkv),
        lambda merged: mix_parts(merged, row1_out),
    )
    stream = row_sublayer(
        stream,
        row_count,
        col_count,
        row2_gain,
        lambda normed_rows: project_parts(normed_rows, row2_qkv),
        lambda merged: mix_parts(merged, row2_out),
    )
    return stream.reshape(images.shape)


def solution(mesh):
    in_specs = (
        P(("batch", "view"), "band", None, None),
        P(),
        P(),
        P(),
        P(),
        P("band", None),
        P(None, "band"),
        P(),
        P("band", None),
        P(None, "band"),
    )
    out_specs = P(("batch", "view"), "band", None, None)

    def chosen(*arrays):
        views, shares = mesh.shape["view"], mesh.shape["view"] * mesh.shape["batch"]
        rows = arrays[0].shape[1] // mesh.shape["band"]
        depth = arrays[5].shape[0] // mesh.shape["band"]
        fits = rows % views == 0 and depth % (8 * shares) == 0
        body = local_swapped if fits else local
        return mapped(body)(*arrays)

    def mapped(body):
        return jax.shard_map(
            body, mesh=mesh, in_specs=in_specs, out_specs=out_specs, check_vma=False
        )

    return chosen
```

```python
import functools

import jax
import jax.numpy as jnp
from jax import lax
from jax.experimental import pallas as pl
from jax.experimental.pallas import tpu as pltpu
from jax.sharding import PartitionSpec as P

HEAD_DIM = 64


EPSILON = 1e-06
BLOCK_ROWS = 512


def rms_normed(stream, gain):
    values = stream.astype(jnp.float32)
    factor = lax.rsqrt(jnp.mean(values * values, axis=-1, keepdims=True) + EPSILON)
    return (values * factor * gain).astype(jnp.bfloat16)


def online_update(carry, queries, keys, values):
    running, total, accum = carry
    scores = jnp.einsum(
        "qhd,khd->hqk", queries, keys, preferred_element_type=jnp.float32
    ) * HEAD_DIM ** (-0.5)
    highest = jnp.maximum(running, jnp.max(scores, axis=-1))
    weights = jnp.exp(scores - highest[:, :, None])
    total = jnp.sum(weights, axis=-1)
    mixed = jnp.einsum(
        "hqk,khd->qhd", weights.astype(jnp.bfloat16), values, preferred_element_type=jnp.float32
    )
    accum = mixed
    return (highest, total, accum)


def unit_attention(trio):
    queries, keys, values = trio
    length, pair_width = queries.shape
    block = min(BLOCK_ROWS, length)
    keys = keys.reshape(length, 2, HEAD_DIM)
    values = values.reshape(length, 2, HEAD_DIM)
    blocks = queries.reshape(length // block, block, 2, HEAD_DIM)

    def one_block(query_block):
        scores = jnp.einsum(
            "qhd,khd->hqk", query_block, keys, preferred_element_type=jnp.float32
        ) * HEAD_DIM ** (-0.5)
        weights = jnp.exp(scores - jnp.max(scores, axis=-1, keepdims=True))
        mixed = jnp.einsum(
            "hqk,khd->qhd", weights.astype(jnp.bfloat16), values, preferred_element_type=jnp.float32
        )
        total = jnp.transpose(jnp.sum(weights, axis=-1))
        return (mixed / total[:, :, None]).astype(jnp.bfloat16).reshape(block, pair_width)

    return lax.map(one_block, blocks).reshape(length, pair_width)


def attend_units(pieces):
    queries, keys, values = pieces
    attended = lax.map(unit_attention, (queries[0], keys[0], values[0]))
    return lax.all_to_all(attended[None], "view", split_axis=2, concat_axis=0, tiled=True)


def project_parts(normed, shard):
    groups = shard.shape[1] // (2 * HEAD_DIM)
    piece = lax.all_gather(shard, "band", axis=0, tiled=True)
    count = piece.shape[0]
    return jnp.einsum(
        "rcd,dpw->rpcw",
        normed,
        piece.reshape(count, groups, 2 * HEAD_DIM),
        preferred_element_type=jnp.float32,
    )


def mix_parts(merged, shard):
    groups = merged.shape[1]
    piece = lax.all_gather(shard, "band", axis=1, tiled=True)
    count = piece.shape[1]
    return jnp.einsum(
        "rpcw,pwn->rcn",
        merged,
        piece.reshape(groups, 2 * HEAD_DIM, count),
        preferred_element_type=jnp.float32,
    )


def row_sublayer(stream, row_count, col_count, gain, project, mix):
    width = stream.shape[1]
    normed = rms_normed(stream, gain).reshape(row_count, col_count, width)
    projected = project(normed)
    groups = projected.shape[1] // 3
    views = lax.axis_size("view")

    def unit_layout(section):
        return section.astype(jnp.bfloat16).reshape(
            views, row_count * groups // views, col_count, 2 * HEAD_DIM
        )

    triple = (
        unit_layout(projected[:, :groups]),
        unit_layout(projected[:, groups : 2 * groups]),
        unit_layout(projected[:, 2 * groups :]),
    )
    returned = attend_units(
        (
            lax.all_to_all(triple[0], "view", split_axis=0, concat_axis=2, tiled=True),
            lax.all_to_all(triple[1], "view", split_axis=0, concat_axis=2, tiled=True),
            lax.all_to_all(triple[2], "view", split_axis=0, concat_axis=2, tiled=True),
        )
    )
    merged = returned.reshape(row_count, groups, col_count, 2 * HEAD_DIM)
    update = mix(merged).reshape(row_count * col_count, width)
    return (stream.astype(jnp.float32) + update).astype(jnp.bfloat16)


def attend_pair(queries, keys, values, mask):
    lane = lax.broadcasted_iota(jnp.int32, queries.shape, 1)
    sides = []
    for side in range(2):
        own = (lane >= side * HEAD_DIM) & (lane < (side + 1) * HEAD_DIM)
        scores = lax.dot_general(
            jnp.where(own, queries, jnp.zeros_like(queries)),
            keys,
            (((1,), (1,)), ((), ())),
            preferred_element_type=jnp.float32,
        ) * HEAD_DIM ** (-0.5)
        if mask is not None:
            scores = jnp.where(mask, scores, -jnp.inf)
        weights = jnp.exp(scores - jnp.max(scores, axis=-1, keepdims=True))
        total = jnp.sum(weights, axis=-1, keepdims=True)
        mixed = jnp.dot(weights.astype(jnp.bfloat16), values, preferred_element_type=jnp.float32)
        sides.append(mixed / total)
    return jnp.where(lane < HEAD_DIM, sides[0], sides[1]).astype(jnp.bfloat16)


def row_layer(stream, gain, weights, inner, mask):
    pair = 2 * HEAD_DIM
    normed = rms_normed(stream, gain)
    projected = jnp.dot(normed, weights[:, : 3 * inner], preferred_element_type=jnp.float32)
    projected = projected.astype(jnp.bfloat16)
    parts = []
    for at in range(0, inner, pair):
        parts.append(
            attend_pair(
                projected[:, at : at + pair],
                projected[:, inner + at : inner + at + pair],
                projected[:, 2 * inner + at : 2 * inner + at + pair],
                mask,
            )
        )
    attended = jnp.concatenate(parts, axis=1)
    update = lax.dot_general(
        attended,
        weights[:, 3 * inner :],
        (((1,), (1,)), ((), ())),
        preferred_element_type=jnp.float32,
    )
    return (stream.astype(jnp.float32) + update).astype(jnp.bfloat16)


def row_mask(tokens, rows, cols):
    def row_of(dim):
        at = lax.broadcasted_iota(jnp.int32, (tokens, tokens), dim)
        return lax.rem(lax.div(at, cols), rows)

    return row_of(0) == row_of(1)


def kernel(
    sizes,
    rows,
    cols,
    x_ref,
    frame_gain_ref,
    frame_qkv_ref,
    frame_out_ref,
    gain1_ref,
    part1_ref,
    gain2_ref,
    part2_ref,
    o_ref,
    whole,
    sent,
    got,
    mixed,
    returned,
    stream_ref,
    swapped,
    refined,
    back,
    part_sem,
    spread_send,
    spread_recv,
    hop_send,
    hop_recv,
    trio_send,
    trio_recv,
    mix_send,
    mix_recv,
    swap_send,
    swap_recv,
    back_send,
    back_recv,
):
    views, bands, batches = sizes["view"], sizes["band"], sizes["batch"]
    view, band, batch = lax.axis_index("view"), lax.axis_index("band"), lax.axis_index("batch")
    tokens = x_ref.shape[0]
    inner = frame_out_ref.shape[0]
    pair = inner // bands
    depth = part1_ref.shape[0]
    share = part1_ref.shape[1] // (views * batches)
    chunk = tokens // views

    hops = []
    for axis, at, size in (("view", view, views), ("batch", batch, batches)):
        step = size // 2
        while step:
            bit = lax.rem(lax.div(at, step), 2)
            hops.append((axis, at + step * (1 - 2 * bit), bit))
            step //= 2
    index = 0
    for level, (_, _, bit) in enumerate(hops):
        index = index + bit * 2**level

    def ahead(d):
        return lax.rem(band + d, bands)

    def behind(d):
        return lax.rem(band + bands - d, bands)

    def other(d):
        return lax.rem(view + d, views)

    def remote(src, dst, send, recv, axis, to):
        return pltpu.make_async_remote_copy(
            src_ref=src,
            dst_ref=dst,
            send_sem=send,
            recv_sem=recv,
            device_id={axis: to},
            device_id_type=pl.DeviceIdType.MESH,
        )

    def spread(layer, d):
        columns = pl.ds(pl.multiple_of(index * share, share), share)
        part = part1_ref if layer == 0 else part2_ref
        at = pl.ds(pl.multiple_of(band * depth, depth), depth)
        return remote(
            part.at[:, columns],
            whole.at[layer, at, columns],
            spread_send.at[layer, d - 1],
            spread_recv.at[layer, d - 1],
            "band",
            ahead(d),
        )

    def hop(layer, level, d):
        axis, to, _ = hops[level]
        held = share * 2**level
        columns = pl.ds(pl.multiple_of(lax.div(index, 2**level) * held, held), held)
        at = pl.ds(pl.multiple_of(behind(d) * depth, depth), depth)
        block = whole.at[layer, at, columns]
        return remote(
            block,
            block,
            hop_send.at[layer, level, d - 1],
            hop_recv.at[layer, level, d - 1],
            axis,
            to,
        )

    def trio(d):
        return remote(
            sent.at[ahead(d)], got.at[band], trio_send.at[d - 1], trio_recv.at[d - 1], "band", ahead(d)
        )

    def mix(d):
        return remote(
            mixed.at[ahead(d)],
            returned.at[band],
            mix_send.at[d - 1],
            mix_recv.at[d - 1],
            "band",
            ahead(d),
        )

    def rows_of(at):
        return pl.ds(pl.multiple_of(at * chunk, chunk), chunk)

    def swap(src, dst, send, recv, d):
        return remote(
            src.at[rows_of(other(d))],
            dst.at[rows_of(view)],
            send.at[d - 1],
            recv.at[d - 1],
            "view",
            other(d),
        )

    def pass_on(layer, level):
        for d in range(1, bands):
            if level == 0:
                spread(layer, d).wait_recv()
            else:
                hop(layer, level - 1, d).wait_recv()
            if level < len(hops):
                hop(layer, level, d).start()

    barrier = pltpu.get_barrier_semaphore()
    greeted = 0
    for axis, at, size in (("band", band, bands), ("view", view, views)):
        for d in range(1, size):
            pl.semaphore_signal(
                barrier,
                inc=1,
                device_id={axis: lax.rem(at + d, size)},
                device_id_type=pl.DeviceIdType.MESH,
            )
            greeted += 1
    for axis, to, _ in hops:
        if axis == "batch":
            pl.semaphore_signal(
                barrier, inc=1, device_id={axis: to}, device_id_type=pl.DeviceIdType.MESH
            )
            greeted += 1
    own = pl.ds(pl.multiple_of(band * depth, depth), depth)
    own_parts = [
        pltpu.make_async_copy(part, whole.at[layer, own], part_sem.at[layer])
        for layer, part in enumerate((part1_ref, part2_ref))
    ]
    for copy in own_parts:
        copy.start()
    normed = rms_normed(x_ref[...], frame_gain_ref[...])
    projected = jnp.dot(normed, frame_qkv_ref[...], preferred_element_type=jnp.float32)
    projected = projected.astype(jnp.bfloat16)
    for t in range(bands):
        for which in range(3):
            at = which * inner + t * pair
            sent[t, :, which * pair : (which + 1) * pair] = projected[:, at : at + pair]
    pl.semaphore_wait(barrier, greeted)

    for d in range(1, bands):
        spread(0, d).start()
    for d in range(1, bands):
        trio(d).start()
    for d in range(1, bands):
        spread(1, d).start()
    got[band] = sent[band]
    pass_on(0, 0)
    pass_on(0, 1)

    for d in range(1, bands):
        trio(d).wait_recv()
    everyone = got[...].reshape(bands * tokens, 3 * pair)

    def attend(at):
        queries = got[at]
        parts = []
        for lo in range(0, pair, 2 * HEAD_DIM):
            hi = lo + 2 * HEAD_DIM
            parts.append(
                attend_pair(
                    queries[:, lo:hi],
                    everyone[:, pair + lo : pair + hi],
                    everyone[:, 2 * pair + lo : 2 * pair + hi],
                    None,
                )
            )
        return jnp.concatenate(parts, axis=1) if len(parts) > 1 else parts[0]

    for d in range(1, bands):
        mixed[ahead(d)] = attend(ahead(d))
        mix(d).start()
    returned[band] = attend(band)
    for level in range(2, len(hops)):
        pass_on(0, level)
    pass_on(1, 0)
    for d in range(1, bands):
        mix(d).wait_recv()
    attended = jnp.concatenate([returned[t] for t in range(bands)], axis=1)
    update = jnp.dot(attended, frame_out_ref[...], preferred_element_type=jnp.float32)
    stream_ref[...] = (x_ref[...].astype(jnp.float32) + update).astype(jnp.bfloat16)
    for d in range(1, views):
        swap(stream_ref, swapped, swap_send, swap_recv, d).start()
    swapped[rows_of(view)] = stream_ref[rows_of(view)]
    pass_on(1, 1)
    for d in range(1, views):
        swap(stream_ref, swapped, swap_send, swap_recv, d).wait_recv()
    for copy in own_parts:
        copy.wait()
    pass_on(0, len(hops))
    mask = row_mask(tokens, rows, cols)
    stream = row_layer(swapped[...], gain1_ref[...], whole.at[0], inner, mask)
    for level in range(2, len(hops) + 1):
        pass_on(1, level)
    refined[...] = row_layer(stream, gain2_ref[...], whole.at[1], inner, mask)
    for d in range(1, views):
        swap(refined, back, back_send, back_recv, d).start()
    back[rows_of(view)] = refined[rows_of(view)]
    for d in range(1, bands):
        for layer in range(2):
            spread(layer, d).wait_send()
            for level in range(len(hops)):
                hop(layer, level, d).wait_send()
        trio(d).wait_send()
        mix(d).wait_send()
    for d in range(1, views):
        swap(stream_ref, swapped, swap_send, swap_recv, d).wait_send()
        swap(refined, back, back_send, back_recv, d).wait()
    o_ref[...] = back[...]


def local_swapped(
    sizes,
    images,
    frame_gain,
    frame_qkv,
    frame_out,
    row1_gain,
    row1_qkv,
    row1_out,
    row2_gain,
    row2_qkv,
    row2_out,
):
    _, row_count, col_count, width = images.shape
    inner = frame_out.shape[0]
    tokens = row_count * col_count
    views, bands, batches = sizes["view"], sizes["band"], sizes["batch"]
    depth = row1_qkv.shape[0]
    pair = inner // bands
    hops = (views * batches).bit_length() - 1
    vmem = pl.BlockSpec(memory_space=pltpu.VMEM)
    part1 = jnp.concatenate([row1_qkv, row1_out.T], axis=1)
    part2 = jnp.concatenate([row2_qkv, row2_out.T], axis=1)
    kind = jnp.bfloat16
    dma = pltpu.SemaphoreType.DMA
    refined = pl.pallas_call(
        functools.partial(kernel, sizes, row_count // views, col_count),
        out_shape=jax.ShapeDtypeStruct((tokens, width), kind),
        in_specs=[vmem] * 8,
        out_specs=vmem,
        scratch_shapes=[
            pltpu.VMEM((2, bands * depth, 4 * inner), kind),
            pltpu.VMEM((bands, tokens, 3 * pair), kind),
            pltpu.VMEM((bands, tokens, 3 * pair), kind),
            pltpu.VMEM((bands, tokens, pair), kind),
            pltpu.VMEM((bands, tokens, pair), kind),
            pltpu.VMEM((tokens, width), kind),
            pltpu.VMEM((tokens, width), kind),
            pltpu.VMEM((tokens, width), kind),
            pltpu.VMEM((tokens, width), kind),
            dma((2,)),
            dma((2, bands - 1)),
            dma((2, bands - 1)),
            dma((2, hops, bands - 1)),
            dma((2, hops, bands - 1)),
            dma((bands - 1,)),
            dma((bands - 1,)),
            dma((bands - 1,)),
            dma((bands - 1,)),
            dma((views - 1,)),
            dma((views - 1,)),
            dma((views - 1,)),
            dma((views - 1,)),
        ],
        compiler_params=pltpu.CompilerParams(
            collective_id=0, has_side_effects=True, vmem_limit_bytes=48 * 1024 * 1024
        ),
    )(
        images.reshape(tokens, width),
        frame_gain[None],
        frame_qkv,
        frame_out,
        row1_gain[None],
        part1,
        row2_gain[None],
        part2,
    )
    return refined.reshape(images.shape)


def local(
    images,
    frame_gain,
    frame_qkv,
    frame_out,
    row1_gain,
    row1_qkv,
    row1_out,
    row2_gain,
    row2_qkv,
    row2_out,
):
    _, row_count, col_count, width = images.shape
    inner = frame_out.shape[0]
    heads = inner // HEAD_DIM
    tokens = row_count * col_count
    stream = images.reshape(tokens, width)
    normed = rms_normed(stream, frame_gain)
    start_state = (
        jnp.full((heads, tokens), -1e30, jnp.float32),
        jnp.zeros((heads, tokens), jnp.float32),
        jnp.zeros((tokens, heads, HEAD_DIM), jnp.float32),
    )
    queries = (
        jnp.dot(normed, frame_qkv[:, :inner], preferred_element_type=jnp.float32)
        .astype(jnp.bfloat16)
        .reshape(tokens, heads, HEAD_DIM)
    )
    piece = lax.all_gather(normed, "band", axis=0, tiled=True)
    count = piece.shape[0]
    paired = jnp.dot(piece, frame_qkv[:, inner:], preferred_element_type=jnp.float32).astype(
        jnp.bfloat16
    )
    result = online_update(
        start_state,
        queries,
        paired[:, :inner].reshape(count, heads, HEAD_DIM),
        paired[:, inner:].reshape(count, heads, HEAD_DIM),
    )
    _, total, accum = result
    attended = (
        (accum / jnp.transpose(total)[:, :, None]).astype(jnp.bfloat16).reshape(tokens, inner)
    )
    update = jnp.dot(attended, frame_out, preferred_element_type=jnp.float32)
    stream = (stream.astype(jnp.float32) + update).astype(jnp.bfloat16)
    stream = row_sublayer(
        stream,
        row_count,
        col_count,
        row1_gain,
        lambda normed_rows: project_parts(normed_rows, row1_qkv),
        lambda merged: mix_parts(merged, row1_out),
    )
    stream = row_sublayer(
        stream,
        row_count,
        col_count,
        row2_gain,
        lambda normed_rows: project_parts(normed_rows, row2_qkv),
        lambda merged: mix_parts(merged, row2_out),
    )
    return stream.reshape(images.shape)


def solution(mesh):
    in_specs = (
        P(("batch", "view"), "band", None, None),
        P(),
        P(),
        P(),
        P(),
        P("band", None),
        P(None, "band"),
        P(),
        P("band", None),
        P(None, "band"),
    )
    out_specs = P(("batch", "view"), "band", None, None)

    sizes = {name: mesh.shape[name] for name in ("view", "band", "batch")}

    def fits(images, frame_out, row_qkv):
        views, bands, batches = sizes["view"], sizes["band"], sizes["batch"]
        rows = images.shape[1] // bands
        inner, width = frame_out.shape
        depth = row_qkv.shape[0] // bands
        if min(views, bands, batches) < 2 or rows % views:
            return False
        return (
            views & (views - 1) == 0
            and batches & (batches - 1) == 0
            and images.shape[0] == views * batches
            and rows * images.shape[2] // views % 16 == 0
            and depth % 16 == 0
            and width == row_qkv.shape[0]
            and inner % (bands * 2 * HEAD_DIM) == 0
            and 4 * inner % (128 * views * batches) == 0
        )

    def chosen(*arrays):
        fit = fits(arrays[0], arrays[3], arrays[5])
        body = functools.partial(local_swapped, sizes) if fit else local
        return jax.shard_map(
            body, mesh=mesh, in_specs=in_specs, out_specs=out_specs, check_vma=False
        )(*arrays)

    return chosen
```

```python
import functools

import jax
import jax.numpy as jnp
from jax import lax
from jax.experimental import pallas as pl
from jax.experimental.pallas import tpu as pltpu
from jax.sharding import PartitionSpec as P

HEAD_DIM = 64


EPSILON = 1e-06
BLOCK_ROWS = 512


def rms_normed(stream, gain):
    values = stream.astype(jnp.float32)
    factor = lax.rsqrt(jnp.mean(values * values, axis=-1, keepdims=True) + EPSILON)
    return (values * factor * gain).astype(jnp.bfloat16)


def online_update(carry, queries, keys, values):
    running, total, accum = carry
    scores = jnp.einsum(
        "qhd,khd->hqk", queries, keys, preferred_element_type=jnp.float32
    ) * HEAD_DIM ** (-0.5)
    highest = jnp.maximum(running, jnp.max(scores, axis=-1))
    weights = jnp.exp(scores - highest[:, :, None])
    total = jnp.sum(weights, axis=-1)
    mixed = jnp.einsum(
        "hqk,khd->qhd", weights.astype(jnp.bfloat16), values, preferred_element_type=jnp.float32
    )
    accum = mixed
    return (highest, total, accum)


def unit_attention(trio):
    queries, keys, values = trio
    length, pair_width = queries.shape
    block = min(BLOCK_ROWS, length)
    keys = keys.reshape(length, 2, HEAD_DIM)
    values = values.reshape(length, 2, HEAD_DIM)
    blocks = queries.reshape(length // block, block, 2, HEAD_DIM)

    def one_block(query_block):
        scores = jnp.einsum(
            "qhd,khd->hqk", query_block, keys, preferred_element_type=jnp.float32
        ) * HEAD_DIM ** (-0.5)
        weights = jnp.exp(scores - jnp.max(scores, axis=-1, keepdims=True))
        mixed = jnp.einsum(
            "hqk,khd->qhd", weights.astype(jnp.bfloat16), values, preferred_element_type=jnp.float32
        )
        total = jnp.transpose(jnp.sum(weights, axis=-1))
        return (mixed / total[:, :, None]).astype(jnp.bfloat16).reshape(block, pair_width)

    return lax.map(one_block, blocks).reshape(length, pair_width)


def attend_units(pieces):
    queries, keys, values = pieces
    attended = lax.map(unit_attention, (queries[0], keys[0], values[0]))
    return lax.all_to_all(attended[None], "view", split_axis=2, concat_axis=0, tiled=True)


def project_parts(normed, shard):
    groups = shard.shape[1] // (2 * HEAD_DIM)
    piece = lax.all_gather(shard, "band", axis=0, tiled=True)
    count = piece.shape[0]
    return jnp.einsum(
        "rcd,dpw->rpcw",
        normed,
        piece.reshape(count, groups, 2 * HEAD_DIM),
        preferred_element_type=jnp.float32,
    )


def mix_parts(merged, shard):
    groups = merged.shape[1]
    piece = lax.all_gather(shard, "band", axis=1, tiled=True)
    count = piece.shape[1]
    return jnp.einsum(
        "rpcw,pwn->rcn",
        merged,
        piece.reshape(groups, 2 * HEAD_DIM, count),
        preferred_element_type=jnp.float32,
    )


def row_sublayer(stream, row_count, col_count, gain, project, mix):
    width = stream.shape[1]
    normed = rms_normed(stream, gain).reshape(row_count, col_count, width)
    projected = project(normed)
    groups = projected.shape[1] // 3
    views = lax.axis_size("view")

    def unit_layout(section):
        return section.astype(jnp.bfloat16).reshape(
            views, row_count * groups // views, col_count, 2 * HEAD_DIM
        )

    triple = (
        unit_layout(projected[:, :groups]),
        unit_layout(projected[:, groups : 2 * groups]),
        unit_layout(projected[:, 2 * groups :]),
    )
    returned = attend_units(
        (
            lax.all_to_all(triple[0], "view", split_axis=0, concat_axis=2, tiled=True),
            lax.all_to_all(triple[1], "view", split_axis=0, concat_axis=2, tiled=True),
            lax.all_to_all(triple[2], "view", split_axis=0, concat_axis=2, tiled=True),
        )
    )
    merged = returned.reshape(row_count, groups, col_count, 2 * HEAD_DIM)
    update = mix(merged).reshape(row_count * col_count, width)
    return (stream.astype(jnp.float32) + update).astype(jnp.bfloat16)


def attend_pair(queries, keys, values, mask):
    lane = lax.broadcasted_iota(jnp.int32, queries.shape, 1)
    sides = []
    for side in range(2):
        own = (lane >= side * HEAD_DIM) & (lane < (side + 1) * HEAD_DIM)
        scores = lax.dot_general(
            jnp.where(own, queries, jnp.zeros_like(queries)),
            keys,
            (((1,), (1,)), ((), ())),
            preferred_element_type=jnp.float32,
        ) * HEAD_DIM ** (-0.5)
        if mask is not None:
            scores = jnp.where(mask, scores, -jnp.inf)
        weights = jnp.exp(scores - jnp.max(scores, axis=-1, keepdims=True))
        total = jnp.sum(weights, axis=-1, keepdims=True)
        mixed = jnp.dot(weights.astype(jnp.bfloat16), values, preferred_element_type=jnp.float32)
        sides.append(mixed / total)
    return jnp.where(lane < HEAD_DIM, sides[0], sides[1]).astype(jnp.bfloat16)


def row_layer(stream, gain, weights, inner, mask):
    pair = 2 * HEAD_DIM
    normed = rms_normed(stream, gain)
    projected = jnp.dot(normed, weights[:, : 3 * inner], preferred_element_type=jnp.float32)
    projected = projected.astype(jnp.bfloat16)
    parts = []
    for at in range(0, inner, pair):
        parts.append(
            attend_pair(
                projected[:, at : at + pair],
                projected[:, inner + at : inner + at + pair],
                projected[:, 2 * inner + at : 2 * inner + at + pair],
                mask,
            )
        )
    attended = jnp.concatenate(parts, axis=1)
    update = lax.dot_general(
        attended,
        weights[:, 3 * inner :],
        (((1,), (1,)), ((), ())),
        preferred_element_type=jnp.float32,
    )
    return (stream.astype(jnp.float32) + update).astype(jnp.bfloat16)


def row_mask(tokens, rows, cols):
    def row_of(dim):
        at = lax.broadcasted_iota(jnp.int32, (tokens, tokens), dim)
        return lax.rem(lax.div(at, cols), rows)

    return row_of(0) == row_of(1)


def kernel(
    sizes,
    rows,
    cols,
    x_ref,
    frame_gain_ref,
    frame_qkv_ref,
    frame_out_ref,
    gain1_ref,
    part1_ref,
    gain2_ref,
    part2_ref,
    o_ref,
    whole,
    sent,
    got,
    mixed,
    returned,
    stream_ref,
    swapped,
    refined,
    back,
    part_sem,
    spread_send,
    spread_recv,
    hop_send,
    hop_recv,
    trio_send,
    trio_recv,
    mix_send,
    mix_recv,
    swap_send,
    swap_recv,
    back_send,
    back_recv,
):
    views, bands, batches = sizes["view"], sizes["band"], sizes["batch"]
    view, band, batch = lax.axis_index("view"), lax.axis_index("band"), lax.axis_index("batch")
    tokens = x_ref.shape[0]
    inner = frame_out_ref.shape[0]
    pair = inner // bands
    depth = part1_ref.shape[0]
    share = part1_ref.shape[1] // (views * batches)
    chunk = tokens // views

    hops = []
    for axis, at, size in (("view", view, views), ("batch", batch, batches)):
        step = size // 2
        while step:
            bit = lax.rem(lax.div(at, step), 2)
            hops.append((axis, at + step * (1 - 2 * bit), bit))
            step //= 2
    streams = [hops, hops[1::-1] + hops[2:]]
    half = depth // len(streams)
    indices = []
    for order in streams:
        index = 0
        for level, (_, _, bit) in enumerate(order):
            index = index + bit * 2**level
        indices.append(index)

    def ahead(d):
        return lax.rem(band + d, bands)

    def behind(d):
        return lax.rem(band + bands - d, bands)

    def other(d):
        return lax.rem(view + d, views)

    def remote(src, dst, send, recv, axis, to):
        return pltpu.make_async_remote_copy(
            src_ref=src,
            dst_ref=dst,
            send_sem=send,
            recv_sem=recv,
            device_id={axis: to},
            device_id_type=pl.DeviceIdType.MESH,
        )

    def share_at(layer, stream, k):
        at = pl.ds(pl.multiple_of(behind(k) * depth + stream * half, half), half)
        columns = pl.ds(pl.multiple_of(indices[stream] * share, share), share)
        return whole.at[layer, at, columns]

    def spread_own(layer, stream, toward):
        part = part1_ref if layer == 0 else part2_ref
        columns = pl.ds(pl.multiple_of(indices[stream] * share, share), share)
        return remote(
            part.at[stream * half : (stream + 1) * half, columns],
            share_at(layer, stream, 0),
            spread_send.at[layer, stream, 0 if toward == 1 else 1],
            spread_recv.at[layer, stream, 0 if toward == 1 else bands - 2],
            "band",
            band + toward,
        )

    def spread_on(layer, stream, k, toward):
        block = share_at(layer, stream, k)
        return remote(
            block,
            block,
            spread_send.at[layer, stream, 1 + k],
            spread_recv.at[layer, stream, k if toward == 1 else k - 2],
            "band",
            band + toward,
        )

    def spread_arrived(layer, stream, k):
        block = share_at(layer, stream, k)
        remote(
            block,
            block,
            spread_send.at[layer, stream, 0],
            spread_recv.at[layer, stream, k - 1],
            "band",
            ahead(1),
        ).wait_recv()

    def own_sends(layer, act):
        for stream in range(len(streams)):
            for toward, there in ((1, band < bands - 1), (-1, band > 0)):

                @pl.when(there)
                def _():
                    act(spread_own(layer, stream, toward))

    def forwards(layer, stream, k, act):
        @pl.when((k <= band) & (band < bands - 1))
        def _():
            act(spread_on(layer, stream, k, 1))

        @pl.when((k > band) & (band > 0))
        def _():
            act(spread_on(layer, stream, k, -1))

    def nearest(t):
        middle = (t + 1) // 2 if t % 2 else bands - t // 2
        return jnp.where(band == 0, bands - t, jnp.where(band == bands - 1, t, middle))

    def hop(layer, stream, level, k):
        axis, to, _ = streams[stream][level]
        held = share * 2**level
        at = pl.ds(pl.multiple_of(behind(k) * depth + stream * half, half), half)
        columns = pl.ds(
            pl.multiple_of(lax.div(indices[stream], 2**level) * held, held), held
        )
        block = whole.at[layer, at, columns]
        return remote(
            block,
            block,
            hop_send.at[layer, stream, level, k - 1],
            hop_recv.at[layer, stream, level, k - 1],
            axis,
            to,
        )

    def trio(d):
        return remote(
            sent.at[ahead(d)], got.at[band], trio_send.at[d - 1], trio_recv.at[d - 1], "band", ahead(d)
        )

    def mix(d):
        return remote(
            mixed.at[ahead(d)],
            returned.at[band],
            mix_send.at[d - 1],
            mix_recv.at[d - 1],
            "band",
            ahead(d),
        )

    def rows_of(at):
        return pl.ds(pl.multiple_of(at * chunk, chunk), chunk)

    def swap(src, dst, send, recv, d):
        return remote(
            src.at[rows_of(other(d))],
            dst.at[rows_of(view)],
            send.at[d - 1],
            recv.at[d - 1],
            "view",
            other(d),
        )

    def pass_on(layer, level):
        for t in range(1, bands):
            k = nearest(t)
            for stream in range(len(streams)):
                if level == 0:
                    spread_arrived(layer, stream, k)
                    forwards(layer, stream, k, lambda copy: copy.start())
                else:
                    hop(layer, stream, level - 1, k).wait_recv()
                if level < len(hops):
                    hop(layer, stream, level, k).start()

    barrier = pltpu.get_barrier_semaphore()
    greeted = 0
    for axis, at, size in (("band", band, bands), ("view", view, views)):
        for d in range(1, size):
            pl.semaphore_signal(
                barrier,
                inc=1,
                device_id={axis: lax.rem(at + d, size)},
                device_id_type=pl.DeviceIdType.MESH,
            )
            greeted += 1
    for axis, to, _ in hops:
        if axis == "batch":
            pl.semaphore_signal(
                barrier, inc=1, device_id={axis: to}, device_id_type=pl.DeviceIdType.MESH
            )
            greeted += 1
    own = pl.ds(pl.multiple_of(band * depth, depth), depth)
    own_parts = [
        pltpu.make_async_copy(part, whole.at[layer, own], part_sem.at[layer])
        for layer, part in enumerate((part1_ref, part2_ref))
    ]
    for copy in own_parts:
        copy.start()
    normed = rms_normed(x_ref[...], frame_gain_ref[...])
    pl.semaphore_wait(barrier, greeted)
    own_sends(0, lambda copy: copy.start())
    projected = jnp.dot(normed, frame_qkv_ref[...], preferred_element_type=jnp.float32)
    projected = projected.astype(jnp.bfloat16)
    for t in range(bands):
        for which in range(3):
            at = which * inner + t * pair
            sent[t, :, which * pair : (which + 1) * pair] = projected[:, at : at + pair]
    for d in range(1, bands):
        trio(d).start()
    own_sends(1, lambda copy: copy.start())
    got[band] = sent[band]
    pass_on(0, 0)
    pass_on(0, 1)

    for d in range(1, bands):
        trio(d).wait_recv()
    everyone = got[...].reshape(bands * tokens, 3 * pair)

    def attend(at):
        queries = got[at]
        parts = []
        for lo in range(0, pair, 2 * HEAD_DIM):
            hi = lo + 2 * HEAD_DIM
            parts.append(
                attend_pair(
                    queries[:, lo:hi],
                    everyone[:, pair + lo : pair + hi],
                    everyone[:, 2 * pair + lo : 2 * pair + hi],
                    None,
                )
            )
        return jnp.concatenate(parts, axis=1) if len(parts) > 1 else parts[0]

    for d in range(1, bands):
        mixed[ahead(d)] = attend(ahead(d))
        mix(d).start()
    returned[band] = attend(band)
    for level in range(2, len(hops)):
        pass_on(0, level)
    pass_on(1, 0)
    for d in range(1, bands):
        mix(d).wait_recv()
    attended = jnp.concatenate([returned[t] for t in range(bands)], axis=1)
    update = jnp.dot(attended, frame_out_ref[...], preferred_element_type=jnp.float32)
    stream_ref[...] = (x_ref[...].astype(jnp.float32) + update).astype(jnp.bfloat16)
    for d in range(1, views):
        swap(stream_ref, swapped, swap_send, swap_recv, d).start()
    swapped[rows_of(view)] = stream_ref[rows_of(view)]
    pass_on(1, 1)
    for d in range(1, views):
        swap(stream_ref, swapped, swap_send, swap_recv, d).wait_recv()
    for copy in own_parts:
        copy.wait()
    pass_on(0, len(hops))
    mask = row_mask(tokens, rows, cols)
    stream = row_layer(swapped[...], gain1_ref[...], whole.at[0], inner, mask)
    for level in range(2, len(hops) + 1):
        pass_on(1, level)
    refined[...] = row_layer(stream, gain2_ref[...], whole.at[1], inner, mask)
    for d in range(1, views):
        swap(refined, back, back_send, back_recv, d).start()
    back[rows_of(view)] = refined[rows_of(view)]
    for layer in range(2):
        own_sends(layer, lambda copy: copy.wait_send())
    for d in range(1, bands):
        for layer in range(2):
            for stream in range(len(streams)):
                forwards(layer, stream, d, lambda copy: copy.wait_send())
                for level in range(len(hops)):
                    hop(layer, stream, level, d).wait_send()
        trio(d).wait_send()
        mix(d).wait_send()
    for d in range(1, views):
        swap(stream_ref, swapped, swap_send, swap_recv, d).wait_send()
        swap(refined, back, back_send, back_recv, d).wait()
    o_ref[...] = back[...]


def local_swapped(
    sizes,
    images,
    frame_gain,
    frame_qkv,
    frame_out,
    row1_gain,
    row1_qkv,
    row1_out,
    row2_gain,
    row2_qkv,
    row2_out,
):
    _, row_count, col_count, width = images.shape
    inner = frame_out.shape[0]
    tokens = row_count * col_count
    views, bands, batches = sizes["view"], sizes["band"], sizes["batch"]
    depth = row1_qkv.shape[0]
    pair = inner // bands
    hops = (views * batches).bit_length() - 1
    vmem = pl.BlockSpec(memory_space=pltpu.VMEM)
    part1 = jnp.concatenate([row1_qkv, row1_out.T], axis=1)
    part2 = jnp.concatenate([row2_qkv, row2_out.T], axis=1)
    kind = jnp.bfloat16
    dma = pltpu.SemaphoreType.DMA
    refined = pl.pallas_call(
        functools.partial(kernel, sizes, row_count // views, col_count),
        out_shape=jax.ShapeDtypeStruct((tokens, width), kind),
        in_specs=[vmem] * 8,
        out_specs=vmem,
        scratch_shapes=[
            pltpu.VMEM((2, bands * depth, 4 * inner), kind),
            pltpu.VMEM((bands, tokens, 3 * pair), kind),
            pltpu.VMEM((bands, tokens, 3 * pair), kind),
            pltpu.VMEM((bands, tokens, pair), kind),
            pltpu.VMEM((bands, tokens, pair), kind),
            pltpu.VMEM((tokens, width), kind),
            pltpu.VMEM((tokens, width), kind),
            pltpu.VMEM((tokens, width), kind),
            pltpu.VMEM((tokens, width), kind),
            dma((2,)),
            dma((2, 2, bands + 1)),
            dma((2, 2, bands - 1)),
            dma((2, 2, hops, bands - 1)),
            dma((2, 2, hops, bands - 1)),
            dma((bands - 1,)),
            dma((bands - 1,)),
            dma((bands - 1,)),
            dma((bands - 1,)),
            dma((views - 1,)),
            dma((views - 1,)),
            dma((views - 1,)),
            dma((views - 1,)),
        ],
        compiler_params=pltpu.CompilerParams(
            collective_id=0, has_side_effects=True, vmem_limit_bytes=48 * 1024 * 1024
        ),
    )(
        images.reshape(tokens, width),
        frame_gain,
        frame_qkv,
        frame_out,
        row1_gain,
        part1,
        row2_gain,
        part2,
    )
    return refined.reshape(images.shape)


def local(
    images,
    frame_gain,
    frame_qkv,
    frame_out,
    row1_gain,
    row1_qkv,
    row1_out,
    row2_gain,
    row2_qkv,
    row2_out,
):
    _, row_count, col_count, width = images.shape
    inner = frame_out.shape[0]
    heads = inner // HEAD_DIM
    tokens = row_count * col_count
    stream = images.reshape(tokens, width)
    normed = rms_normed(stream, frame_gain)
    start_state = (
        jnp.full((heads, tokens), -1e30, jnp.float32),
        jnp.zeros((heads, tokens), jnp.float32),
        jnp.zeros((tokens, heads, HEAD_DIM), jnp.float32),
    )
    queries = (
        jnp.dot(normed, frame_qkv[:, :inner], preferred_element_type=jnp.float32)
        .astype(jnp.bfloat16)
        .reshape(tokens, heads, HEAD_DIM)
    )
    piece = lax.all_gather(normed, "band", axis=0, tiled=True)
    count = piece.shape[0]
    paired = jnp.dot(piece, frame_qkv[:, inner:], preferred_element_type=jnp.float32).astype(
        jnp.bfloat16
    )
    result = online_update(
        start_state,
        queries,
        paired[:, :inner].reshape(count, heads, HEAD_DIM),
        paired[:, inner:].reshape(count, heads, HEAD_DIM),
    )
    _, total, accum = result
    attended = (
        (accum / jnp.transpose(total)[:, :, None]).astype(jnp.bfloat16).reshape(tokens, inner)
    )
    update = jnp.dot(attended, frame_out, preferred_element_type=jnp.float32)
    stream = (stream.astype(jnp.float32) + update).astype(jnp.bfloat16)
    stream = row_sublayer(
        stream,
        row_count,
        col_count,
        row1_gain,
        lambda normed_rows: project_parts(normed_rows, row1_qkv),
        lambda merged: mix_parts(merged, row1_out),
    )
    stream = row_sublayer(
        stream,
        row_count,
        col_count,
        row2_gain,
        lambda normed_rows: project_parts(normed_rows, row2_qkv),
        lambda merged: mix_parts(merged, row2_out),
    )
    return stream.reshape(images.shape)


def solution(mesh):
    in_specs = (
        P(("batch", "view"), "band", None, None),
        P(),
        P(),
        P(),
        P(),
        P("band", None),
        P(None, "band"),
        P(),
        P("band", None),
        P(None, "band"),
    )
    out_specs = P(("batch", "view"), "band", None, None)

    sizes = {name: mesh.shape[name] for name in ("view", "band", "batch")}

    def fits(images, frame_out, row_qkv):
        views, bands, batches = sizes["view"], sizes["band"], sizes["batch"]
        rows = images.shape[1] // bands
        inner, width = frame_out.shape
        depth = row_qkv.shape[0] // bands
        if min(views, bands, batches) < 2 or bands > 4 or rows % views:
            return False
        return (
            views & (views - 1) == 0
            and batches & (batches - 1) == 0
            and images.shape[0] == views * batches
            and rows * images.shape[2] // views % 16 == 0
            and depth % 32 == 0
            and width == row_qkv.shape[0]
            and inner % (bands * 2 * HEAD_DIM) == 0
            and 4 * inner % (128 * views * batches) == 0
        )

    def chosen(*arrays):
        fit = fits(arrays[0], arrays[3], arrays[5])
        body = functools.partial(local_swapped, sizes) if fit else local
        return jax.shard_map(
            body, mesh=mesh, in_specs=in_specs, out_specs=out_specs, check_vma=False
        )(*arrays)

    return chosen
```

```python
import functools

import jax
import jax.numpy as jnp
from jax import lax
from jax.experimental import pallas as pl
from jax.experimental.pallas import tpu as pltpu
from jax.sharding import PartitionSpec as P

HEAD_DIM = 64


EPSILON = 1e-06
BLOCK_ROWS = 512


def rms_normed(stream, gain):
    values = stream.astype(jnp.float32)
    factor = lax.rsqrt(jnp.mean(values * values, axis=-1, keepdims=True) + EPSILON)
    return (values * factor * gain).astype(jnp.bfloat16)


def online_update(carry, queries, keys, values):
    running, total, accum = carry
    scores = jnp.einsum(
        "qhd,khd->hqk", queries, keys, preferred_element_type=jnp.float32
    ) * HEAD_DIM ** (-0.5)
    highest = jnp.maximum(running, jnp.max(scores, axis=-1))
    weights = jnp.exp(scores - highest[:, :, None])
    total = jnp.sum(weights, axis=-1)
    mixed = jnp.einsum(
        "hqk,khd->qhd", weights.astype(jnp.bfloat16), values, preferred_element_type=jnp.float32
    )
    accum = mixed
    return (highest, total, accum)


def unit_attention(trio):
    queries, keys, values = trio
    length, pair_width = queries.shape
    block = min(BLOCK_ROWS, length)
    keys = keys.reshape(length, 2, HEAD_DIM)
    values = values.reshape(length, 2, HEAD_DIM)
    blocks = queries.reshape(length // block, block, 2, HEAD_DIM)

    def one_block(query_block):
        scores = jnp.einsum(
            "qhd,khd->hqk", query_block, keys, preferred_element_type=jnp.float32
        ) * HEAD_DIM ** (-0.5)
        weights = jnp.exp(scores - jnp.max(scores, axis=-1, keepdims=True))
        mixed = jnp.einsum(
            "hqk,khd->qhd", weights.astype(jnp.bfloat16), values, preferred_element_type=jnp.float32
        )
        total = jnp.transpose(jnp.sum(weights, axis=-1))
        return (mixed / total[:, :, None]).astype(jnp.bfloat16).reshape(block, pair_width)

    return lax.map(one_block, blocks).reshape(length, pair_width)


def attend_units(pieces):
    queries, keys, values = pieces
    attended = lax.map(unit_attention, (queries[0], keys[0], values[0]))
    return lax.all_to_all(attended[None], "view", split_axis=2, concat_axis=0, tiled=True)


def project_parts(normed, shard):
    groups = shard.shape[1] // (2 * HEAD_DIM)
    piece = lax.all_gather(shard, "band", axis=0, tiled=True)
    count = piece.shape[0]
    return jnp.einsum(
        "rcd,dpw->rpcw",
        normed,
        piece.reshape(count, groups, 2 * HEAD_DIM),
        preferred_element_type=jnp.float32,
    )


def mix_parts(merged, shard):
    groups = merged.shape[1]
    piece = lax.all_gather(shard, "band", axis=1, tiled=True)
    count = piece.shape[1]
    return jnp.einsum(
        "rpcw,pwn->rcn",
        merged,
        piece.reshape(groups, 2 * HEAD_DIM, count),
        preferred_element_type=jnp.float32,
    )


def row_sublayer(stream, row_count, col_count, gain, project, mix):
    width = stream.shape[1]
    normed = rms_normed(stream, gain).reshape(row_count, col_count, width)
    projected = project(normed)
    groups = projected.shape[1] // 3
    views = lax.axis_size("view")

    def unit_layout(section):
        return section.astype(jnp.bfloat16).reshape(
            views, row_count * groups // views, col_count, 2 * HEAD_DIM
        )

    triple = (
        unit_layout(projected[:, :groups]),
        unit_layout(projected[:, groups : 2 * groups]),
        unit_layout(projected[:, 2 * groups :]),
    )
    returned = attend_units(
        (
            lax.all_to_all(triple[0], "view", split_axis=0, concat_axis=2, tiled=True),
            lax.all_to_all(triple[1], "view", split_axis=0, concat_axis=2, tiled=True),
            lax.all_to_all(triple[2], "view", split_axis=0, concat_axis=2, tiled=True),
        )
    )
    merged = returned.reshape(row_count, groups, col_count, 2 * HEAD_DIM)
    update = mix(merged).reshape(row_count * col_count, width)
    return (stream.astype(jnp.float32) + update).astype(jnp.bfloat16)


def attend_pair(queries, keys, values, mask):
    lane = lax.broadcasted_iota(jnp.int32, queries.shape, 1)
    sides = []
    for side in range(2):
        own = (lane >= side * HEAD_DIM) & (lane < (side + 1) * HEAD_DIM)
        scores = lax.dot_general(
            jnp.where(own, queries, jnp.zeros_like(queries)),
            keys,
            (((1,), (1,)), ((), ())),
            preferred_element_type=jnp.float32,
        ) * HEAD_DIM ** (-0.5)
        if mask is not None:
            scores = jnp.where(mask, scores, -jnp.inf)
        weights = jnp.exp(scores - jnp.max(scores, axis=-1, keepdims=True))
        total = jnp.sum(weights, axis=-1, keepdims=True)
        mixed = jnp.dot(weights.astype(jnp.bfloat16), values, preferred_element_type=jnp.float32)
        sides.append(mixed / total)
    return jnp.where(lane < HEAD_DIM, sides[0], sides[1]).astype(jnp.bfloat16)


def row_layer(stream, gain, weights, inner, mask):
    pair = 2 * HEAD_DIM
    normed = rms_normed(stream, gain)
    projected = jnp.dot(normed, weights[:, : 3 * inner], preferred_element_type=jnp.float32)
    projected = projected.astype(jnp.bfloat16)
    parts = []
    for at in range(0, inner, pair):
        parts.append(
            attend_pair(
                projected[:, at : at + pair],
                projected[:, inner + at : inner + at + pair],
                projected[:, 2 * inner + at : 2 * inner + at + pair],
                mask,
            )
        )
    attended = jnp.concatenate(parts, axis=1)
    update = lax.dot_general(
        attended,
        weights[:, 3 * inner :],
        (((1,), (1,)), ((), ())),
        preferred_element_type=jnp.float32,
    )
    return (stream.astype(jnp.float32) + update).astype(jnp.bfloat16)


def row_mask(tokens, rows, cols):
    def row_of(dim):
        at = lax.broadcasted_iota(jnp.int32, (tokens, tokens), dim)
        return lax.rem(lax.div(at, cols), rows)

    return row_of(0) == row_of(1)


def kernel(
    sizes,
    rows,
    cols,
    x_hbm,
    frame_gain_hbm,
    frame_qkv_hbm,
    frame_out_hbm,
    gain1_hbm,
    qkv1_hbm,
    out1_hbm,
    gain2_hbm,
    qkv2_hbm,
    out2_hbm,
    o_ref,
    x_ref,
    frame_gain_ref,
    frame_qkv_ref,
    frame_out_ref,
    gain1_ref,
    gain2_ref,
    parts,
    load_sem,
    whole,
    sent,
    got,
    mixed,
    returned,
    stream_ref,
    swapped,
    refined,
    back,
    part_sem,
    spread_send,
    spread_recv,
    hop_send,
    hop_recv,
    trio_send,
    trio_recv,
    mix_send,
    mix_recv,
    swap_send,
    swap_recv,
    back_send,
    back_recv,
):
    views, bands, batches = sizes["view"], sizes["band"], sizes["batch"]
    view, band, batch = lax.axis_index("view"), lax.axis_index("band"), lax.axis_index("batch")
    tokens = x_hbm.shape[0]
    inner = frame_out_hbm.shape[0]
    pair = inner // bands
    depth = qkv1_hbm.shape[0]
    share = parts.shape[2] // (views * batches)
    chunk = tokens // views

    hops = []
    for axis, at, size in (("view", view, views), ("batch", batch, batches)):
        step = size // 2
        while step:
            bit = lax.rem(lax.div(at, step), 2)
            hops.append((axis, at + step * (1 - 2 * bit), bit))
            step //= 2
    streams = [hops, hops[1::-1] + hops[2:]]
    half = depth // len(streams)
    indices = []
    for order in streams:
        index = 0
        for level, (_, _, bit) in enumerate(order):
            index = index + bit * 2**level
        indices.append(index)

    def ahead(d):
        return lax.rem(band + d, bands)

    def behind(d):
        return lax.rem(band + bands - d, bands)

    def other(d):
        return lax.rem(view + d, views)

    def remote(src, dst, send, recv, axis, to):
        return pltpu.make_async_remote_copy(
            src_ref=src,
            dst_ref=dst,
            send_sem=send,
            recv_sem=recv,
            device_id={axis: to},
            device_id_type=pl.DeviceIdType.MESH,
        )

    def share_at(layer, stream, k):
        at = pl.ds(pl.multiple_of(behind(k) * depth + stream * half, half), half)
        columns = pl.ds(pl.multiple_of(indices[stream] * share, share), share)
        return whole.at[layer, at, columns]

    def spread_own(layer, stream, toward):
        columns = pl.ds(pl.multiple_of(indices[stream] * share, share), share)
        return remote(
            parts.at[layer, stream * half : (stream + 1) * half, columns],
            share_at(layer, stream, 0),
            spread_send.at[layer, stream, 0 if toward == 1 else 1],
            spread_recv.at[layer, stream, 0 if toward == 1 else bands - 2],
            "band",
            band + toward,
        )

    def spread_on(layer, stream, k, toward):
        block = share_at(layer, stream, k)
        return remote(
            block,
            block,
            spread_send.at[layer, stream, 1 + k],
            spread_recv.at[layer, stream, k if toward == 1 else k - 2],
            "band",
            band + toward,
        )

    def spread_arrived(layer, stream, k):
        block = share_at(layer, stream, k)
        remote(
            block,
            block,
            spread_send.at[layer, stream, 0],
            spread_recv.at[layer, stream, k - 1],
            "band",
            ahead(1),
        ).wait_recv()

    def own_sends(layer, act):
        for stream in range(len(streams)):
            for toward, there in ((1, band < bands - 1), (-1, band > 0)):

                @pl.when(there)
                def _():
                    act(spread_own(layer, stream, toward))

    def forwards(layer, stream, k, act):
        @pl.when((k <= band) & (band < bands - 1))
        def _():
            act(spread_on(layer, stream, k, 1))

        @pl.when((k > band) & (band > 0))
        def _():
            act(spread_on(layer, stream, k, -1))

    def nearest(t):
        middle = (t + 1) // 2 if t % 2 else bands - t // 2
        return jnp.where(band == 0, bands - t, jnp.where(band == bands - 1, t, middle))

    def hop(layer, stream, level, k):
        axis, to, _ = streams[stream][level]
        held = share * 2**level
        at = pl.ds(pl.multiple_of(behind(k) * depth + stream * half, half), half)
        columns = pl.ds(
            pl.multiple_of(lax.div(indices[stream], 2**level) * held, held), held
        )
        block = whole.at[layer, at, columns]
        return remote(
            block,
            block,
            hop_send.at[layer, stream, level, k - 1],
            hop_recv.at[layer, stream, level, k - 1],
            axis,
            to,
        )

    def trio(d):
        return remote(
            sent.at[ahead(d)], got.at[band], trio_send.at[d - 1], trio_recv.at[d - 1], "band", ahead(d)
        )

    def mix(d):
        return remote(
            mixed.at[ahead(d)],
            returned.at[band],
            mix_send.at[d - 1],
            mix_recv.at[d - 1],
            "band",
            ahead(d),
        )

    def rows_of(at):
        return pl.ds(pl.multiple_of(at * chunk, chunk), chunk)

    def swap(src, dst, send, recv, d):
        return remote(
            src.at[rows_of(other(d))],
            dst.at[rows_of(view)],
            send.at[d - 1],
            recv.at[d - 1],
            "view",
            other(d),
        )

    def pass_on(layer, level):
        for t in range(1, bands):
            k = nearest(t)
            for stream in range(len(streams)):
                if level == 0:
                    spread_arrived(layer, stream, k)
                    forwards(layer, stream, k, lambda copy: copy.start())
                else:
                    hop(layer, stream, level - 1, k).wait_recv()
                if level < len(hops):
                    hop(layer, stream, level, k).start()

    loads = {}
    for at, (name, src, dst) in enumerate(
        (
            ("out1", out1_hbm, parts.at[0, :, 3 * inner :]),
            ("qkv1", qkv1_hbm, parts.at[0, :, : 3 * inner]),
            ("x", x_hbm, x_ref),
            ("frame_gain", frame_gain_hbm, frame_gain_ref),
            ("frame_qkv", frame_qkv_hbm, frame_qkv_ref),
            ("out2", out2_hbm, parts.at[1, :, 3 * inner :]),
            ("qkv2", qkv2_hbm, parts.at[1, :, : 3 * inner]),
            ("frame_out", frame_out_hbm, frame_out_ref),
            ("gain1", gain1_hbm, gain1_ref),
            ("gain2", gain2_hbm, gain2_ref),
        )
    ):
        loads[name] = pltpu.make_async_copy(src, dst, load_sem.at[at])

    barrier = pltpu.get_barrier_semaphore()
    greeted = 0
    for axis, at, size in (("band", band, bands), ("view", view, views)):
        for d in range(1, size):
            pl.semaphore_signal(
                barrier,
                inc=1,
                device_id={axis: lax.rem(at + d, size)},
                device_id_type=pl.DeviceIdType.MESH,
            )
            greeted += 1
    for axis, to, _ in hops:
        if axis == "batch":
            pl.semaphore_signal(
                barrier, inc=1, device_id={axis: to}, device_id_type=pl.DeviceIdType.MESH
            )
            greeted += 1
    own = pl.ds(pl.multiple_of(band * depth, depth), depth)
    for copy in loads.values():
        copy.start()
    own_parts = [
        pltpu.make_async_copy(parts.at[layer], whole.at[layer, own], part_sem.at[layer])
        for layer in range(2)
    ]

    loads["out1"].wait()
    loads["qkv1"].wait()
    pl.semaphore_wait(barrier, greeted)
    own_sends(0, lambda copy: copy.start())
    own_parts[0].start()
    loads["x"].wait()
    loads["frame_gain"].wait()
    normed = rms_normed(x_ref[...], frame_gain_ref[...])
    loads["frame_qkv"].wait()
    projected = jnp.dot(normed, frame_qkv_ref[...], preferred_element_type=jnp.float32)
    projected = projected.astype(jnp.bfloat16)
    for t in range(bands):
        for which in range(3):
            at = which * inner + t * pair
            sent[t, :, which * pair : (which + 1) * pair] = projected[:, at : at + pair]
    for d in range(1, bands):
        trio(d).start()
    loads["out2"].wait()
    loads["qkv2"].wait()
    own_parts[1].start()
    own_sends(1, lambda copy: copy.start())
    got[band] = sent[band]
    pass_on(0, 0)
    pass_on(0, 1)

    for d in range(1, bands):
        trio(d).wait_recv()
    everyone = got[...].reshape(bands * tokens, 3 * pair)

    def attend(at):
        queries = got[at]
        parts = []
        for lo in range(0, pair, 2 * HEAD_DIM):
            hi = lo + 2 * HEAD_DIM
            parts.append(
                attend_pair(
                    queries[:, lo:hi],
                    everyone[:, pair + lo : pair + hi],
                    everyone[:, 2 * pair + lo : 2 * pair + hi],
                    None,
                )
            )
        return jnp.concatenate(parts, axis=1) if len(parts) > 1 else parts[0]

    for d in range(1, bands):
        mixed[ahead(d)] = attend(ahead(d))
        mix(d).start()
    returned[band] = attend(band)
    for level in range(2, len(hops)):
        pass_on(0, level)
    pass_on(1, 0)
    for d in range(1, bands):
        mix(d).wait_recv()
    for name in ("frame_out", "gain1", "gain2"):
        loads[name].wait()
    attended = jnp.concatenate([returned[t] for t in range(bands)], axis=1)
    update = jnp.dot(attended, frame_out_ref[...], preferred_element_type=jnp.float32)
    stream_ref[...] = (x_ref[...].astype(jnp.float32) + update).astype(jnp.bfloat16)
    for d in range(1, views):
        swap(stream_ref, swapped, swap_send, swap_recv, d).start()
    swapped[rows_of(view)] = stream_ref[rows_of(view)]
    pass_on(1, 1)
    for d in range(1, views):
        swap(stream_ref, swapped, swap_send, swap_recv, d).wait_recv()
    for copy in own_parts:
        copy.wait()
    pass_on(0, len(hops))
    mask = row_mask(tokens, rows, cols)
    stream = row_layer(swapped[...], gain1_ref[...], whole.at[0], inner, mask)
    for level in range(2, len(hops) + 1):
        pass_on(1, level)
    refined[...] = row_layer(stream, gain2_ref[...], whole.at[1], inner, mask)
    for d in range(1, views):
        swap(refined, back, back_send, back_recv, d).start()
    back[rows_of(view)] = refined[rows_of(view)]
    for layer in range(2):
        own_sends(layer, lambda copy: copy.wait_send())
    for d in range(1, bands):
        for layer in range(2):
            for stream in range(len(streams)):
                forwards(layer, stream, d, lambda copy: copy.wait_send())
                for level in range(len(hops)):
                    hop(layer, stream, level, d).wait_send()
        trio(d).wait_send()
        mix(d).wait_send()
    for d in range(1, views):
        swap(stream_ref, swapped, swap_send, swap_recv, d).wait_send()
        swap(refined, back, back_send, back_recv, d).wait()
    o_ref[...] = back[...]


def local_swapped(
    sizes,
    images,
    frame_gain,
    frame_qkv,
    frame_out,
    row1_gain,
    row1_qkv,
    row1_out,
    row2_gain,
    row2_qkv,
    row2_out,
):
    _, row_count, col_count, width = images.shape
    inner = frame_out.shape[0]
    tokens = row_count * col_count
    views, bands, batches = sizes["view"], sizes["band"], sizes["batch"]
    depth = row1_qkv.shape[0]
    pair = inner // bands
    hops = (views * batches).bit_length() - 1
    vmem = pl.BlockSpec(memory_space=pltpu.VMEM)
    kind = jnp.bfloat16
    dma = pltpu.SemaphoreType.DMA
    refined = pl.pallas_call(
        functools.partial(kernel, sizes, row_count // views, col_count),
        out_shape=jax.ShapeDtypeStruct((tokens, width), kind),
        in_specs=[pl.BlockSpec(memory_space=pltpu.HBM)] * 10,
        out_specs=vmem,
        scratch_shapes=[
            pltpu.VMEM((tokens, width), kind),
            pltpu.VMEM(frame_gain.shape, frame_gain.dtype),
            pltpu.VMEM(frame_qkv.shape, kind),
            pltpu.VMEM(frame_out.shape, kind),
            pltpu.VMEM(row1_gain.shape, row1_gain.dtype),
            pltpu.VMEM(row2_gain.shape, row2_gain.dtype),
            pltpu.VMEM((2, depth, 4 * inner), kind),
            dma((10,)),
            pltpu.VMEM((2, bands * depth, 4 * inner), kind),
            pltpu.VMEM((bands, tokens, 3 * pair), kind),
            pltpu.VMEM((bands, tokens, 3 * pair), kind),
            pltpu.VMEM((bands, tokens, pair), kind),
            pltpu.VMEM((bands, tokens, pair), kind),
            pltpu.VMEM((tokens, width), kind),
            pltpu.VMEM((tokens, width), kind),
            pltpu.VMEM((tokens, width), kind),
            pltpu.VMEM((tokens, width), kind),
            dma((2,)),
            dma((2, 2, bands + 1)),
            dma((2, 2, bands - 1)),
            dma((2, 2, hops, bands - 1)),
            dma((2, 2, hops, bands - 1)),
            dma((bands - 1,)),
            dma((bands - 1,)),
            dma((bands - 1,)),
            dma((bands - 1,)),
            dma((views - 1,)),
            dma((views - 1,)),
            dma((views - 1,)),
            dma((views - 1,)),
        ],
        compiler_params=pltpu.CompilerParams(
            collective_id=0, has_side_effects=True, vmem_limit_bytes=63 * 1024 * 1024
        ),
    )(
        images.reshape(tokens, width),
        frame_gain,
        frame_qkv,
        frame_out,
        row1_gain,
        row1_qkv,
        row1_out.T,
        row2_gain,
        row2_qkv,
        row2_out.T,
    )
    return refined.reshape(images.shape)


def local(
    images,
    frame_gain,
    frame_qkv,
    frame_out,
    row1_gain,
    row1_qkv,
    row1_out,
    row2_gain,
    row2_qkv,
    row2_out,
):
    _, row_count, col_count, width = images.shape
    inner = frame_out.shape[0]
    heads = inner // HEAD_DIM
    tokens = row_count * col_count
    stream = images.reshape(tokens, width)
    normed = rms_normed(stream, frame_gain)
    start_state = (
        jnp.full((heads, tokens), -1e30, jnp.float32),
        jnp.zeros((heads, tokens), jnp.float32),
        jnp.zeros((tokens, heads, HEAD_DIM), jnp.float32),
    )
    queries = (
        jnp.dot(normed, frame_qkv[:, :inner], preferred_element_type=jnp.float32)
        .astype(jnp.bfloat16)
        .reshape(tokens, heads, HEAD_DIM)
    )
    piece = lax.all_gather(normed, "band", axis=0, tiled=True)
    count = piece.shape[0]
    paired = jnp.dot(piece, frame_qkv[:, inner:], preferred_element_type=jnp.float32).astype(
        jnp.bfloat16
    )
    result = online_update(
        start_state,
        queries,
        paired[:, :inner].reshape(count, heads, HEAD_DIM),
        paired[:, inner:].reshape(count, heads, HEAD_DIM),
    )
    _, total, accum = result
    attended = (
        (accum / jnp.transpose(total)[:, :, None]).astype(jnp.bfloat16).reshape(tokens, inner)
    )
    update = jnp.dot(attended, frame_out, preferred_element_type=jnp.float32)
    stream = (stream.astype(jnp.float32) + update).astype(jnp.bfloat16)
    stream = row_sublayer(
        stream,
        row_count,
        col_count,
        row1_gain,
        lambda normed_rows: project_parts(normed_rows, row1_qkv),
        lambda merged: mix_parts(merged, row1_out),
    )
    stream = row_sublayer(
        stream,
        row_count,
        col_count,
        row2_gain,
        lambda normed_rows: project_parts(normed_rows, row2_qkv),
        lambda merged: mix_parts(merged, row2_out),
    )
    return stream.reshape(images.shape)


def solution(mesh):
    in_specs = (
        P(("batch", "view"), "band", None, None),
        P(),
        P(),
        P(),
        P(),
        P("band", None),
        P(None, "band"),
        P(),
        P("band", None),
        P(None, "band"),
    )
    out_specs = P(("batch", "view"), "band", None, None)

    sizes = {name: mesh.shape[name] for name in ("view", "band", "batch")}

    def fits(images, frame_out, row_qkv):
        views, bands, batches = sizes["view"], sizes["band"], sizes["batch"]
        rows = images.shape[1] // bands
        inner, width = frame_out.shape
        depth = row_qkv.shape[0] // bands
        if min(views, bands, batches) < 2 or bands > 4 or rows % views:
            return False
        return (
            views & (views - 1) == 0
            and batches & (batches - 1) == 0
            and images.shape[0] == views * batches
            and rows * images.shape[2] // views % 16 == 0
            and depth % 32 == 0
            and width == row_qkv.shape[0]
            and inner % (bands * 2 * HEAD_DIM) == 0
            and 4 * inner % (128 * views * batches) == 0
        )

    def chosen(*arrays):
        fit = fits(arrays[0], arrays[3], arrays[5])
        body = functools.partial(local_swapped, sizes) if fit else local
        return jax.shard_map(
            body, mesh=mesh, in_specs=in_specs, out_specs=out_specs, check_vma=False
        )(*arrays)

    return chosen
```

```python
import functools

import jax
import jax.numpy as jnp
from jax import lax
from jax.experimental import pallas as pl
from jax.experimental.pallas import tpu as pltpu
from jax.sharding import PartitionSpec as P

HEAD_DIM = 64


EPSILON = 1e-06
BLOCK_ROWS = 512


def rms_normed(stream, gain):
    values = stream.astype(jnp.float32)
    factor = lax.rsqrt(jnp.mean(values * values, axis=-1, keepdims=True) + EPSILON)
    return (values * factor * gain).astype(jnp.bfloat16)


def online_update(carry, queries, keys, values):
    running, total, accum = carry
    scores = jnp.einsum(
        "qhd,khd->hqk", queries, keys, preferred_element_type=jnp.float32
    ) * HEAD_DIM ** (-0.5)
    highest = jnp.maximum(running, jnp.max(scores, axis=-1))
    weights = jnp.exp(scores - highest[:, :, None])
    total = jnp.sum(weights, axis=-1)
    mixed = jnp.einsum(
        "hqk,khd->qhd", weights.astype(jnp.bfloat16), values, preferred_element_type=jnp.float32
    )
    accum = mixed
    return (highest, total, accum)


def unit_attention(trio):
    queries, keys, values = trio
    length, pair_width = queries.shape
    block = min(BLOCK_ROWS, length)
    keys = keys.reshape(length, 2, HEAD_DIM)
    values = values.reshape(length, 2, HEAD_DIM)
    blocks = queries.reshape(length // block, block, 2, HEAD_DIM)

    def one_block(query_block):
        scores = jnp.einsum(
            "qhd,khd->hqk", query_block, keys, preferred_element_type=jnp.float32
        ) * HEAD_DIM ** (-0.5)
        weights = jnp.exp(scores - jnp.max(scores, axis=-1, keepdims=True))
        mixed = jnp.einsum(
            "hqk,khd->qhd", weights.astype(jnp.bfloat16), values, preferred_element_type=jnp.float32
        )
        total = jnp.transpose(jnp.sum(weights, axis=-1))
        return (mixed / total[:, :, None]).astype(jnp.bfloat16).reshape(block, pair_width)

    return lax.map(one_block, blocks).reshape(length, pair_width)


def attend_units(pieces):
    queries, keys, values = pieces
    attended = lax.map(unit_attention, (queries[0], keys[0], values[0]))
    return lax.all_to_all(attended[None], "view", split_axis=2, concat_axis=0, tiled=True)


def project_parts(normed, shard):
    groups = shard.shape[1] // (2 * HEAD_DIM)
    piece = lax.all_gather(shard, "band", axis=0, tiled=True)
    count = piece.shape[0]
    return jnp.einsum(
        "rcd,dpw->rpcw",
        normed,
        piece.reshape(count, groups, 2 * HEAD_DIM),
        preferred_element_type=jnp.float32,
    )


def mix_parts(merged, shard):
    groups = merged.shape[1]
    piece = lax.all_gather(shard, "band", axis=1, tiled=True)
    count = piece.shape[1]
    return jnp.einsum(
        "rpcw,pwn->rcn",
        merged,
        piece.reshape(groups, 2 * HEAD_DIM, count),
        preferred_element_type=jnp.float32,
    )


def row_sublayer(stream, row_count, col_count, gain, project, mix):
    width = stream.shape[1]
    normed = rms_normed(stream, gain).reshape(row_count, col_count, width)
    projected = project(normed)
    groups = projected.shape[1] // 3
    views = lax.axis_size("view")

    def unit_layout(section):
        return section.astype(jnp.bfloat16).reshape(
            views, row_count * groups // views, col_count, 2 * HEAD_DIM
        )

    triple = (
        unit_layout(projected[:, :groups]),
        unit_layout(projected[:, groups : 2 * groups]),
        unit_layout(projected[:, 2 * groups :]),
    )
    returned = attend_units(
        (
            lax.all_to_all(triple[0], "view", split_axis=0, concat_axis=2, tiled=True),
            lax.all_to_all(triple[1], "view", split_axis=0, concat_axis=2, tiled=True),
            lax.all_to_all(triple[2], "view", split_axis=0, concat_axis=2, tiled=True),
        )
    )
    merged = returned.reshape(row_count, groups, col_count, 2 * HEAD_DIM)
    update = mix(merged).reshape(row_count * col_count, width)
    return (stream.astype(jnp.float32) + update).astype(jnp.bfloat16)


def attend_pair(queries, keys, values, mask):
    lane = lax.broadcasted_iota(jnp.int32, queries.shape, 1)
    sides = []
    for side in range(2):
        own = (lane >= side * HEAD_DIM) & (lane < (side + 1) * HEAD_DIM)
        scores = lax.dot_general(
            jnp.where(own, queries, jnp.zeros_like(queries)),
            keys,
            (((1,), (1,)), ((), ())),
            preferred_element_type=jnp.float32,
        ) * HEAD_DIM ** (-0.5)
        if mask is not None:
            scores = jnp.where(mask, scores, -jnp.inf)
        weights = jnp.exp(scores - jnp.max(scores, axis=-1, keepdims=True))
        total = jnp.sum(weights, axis=-1, keepdims=True)
        mixed = jnp.dot(weights.astype(jnp.bfloat16), values, preferred_element_type=jnp.float32)
        sides.append(mixed / total)
    return jnp.where(lane < HEAD_DIM, sides[0], sides[1]).astype(jnp.bfloat16)


def row_layer(stream, gain, weights, inner, mask):
    pair = 2 * HEAD_DIM
    normed = rms_normed(stream, gain)
    projected = jnp.dot(normed, weights[:, : 3 * inner], preferred_element_type=jnp.float32)
    projected = projected.astype(jnp.bfloat16)
    parts = []
    for at in range(0, inner, pair):
        parts.append(
            attend_pair(
                projected[:, at : at + pair],
                projected[:, inner + at : inner + at + pair],
                projected[:, 2 * inner + at : 2 * inner + at + pair],
                mask,
            )
        )
    attended = jnp.concatenate(parts, axis=1)
    update = lax.dot_general(
        attended,
        weights[:, 3 * inner :],
        (((1,), (1,)), ((), ())),
        preferred_element_type=jnp.float32,
    )
    return (stream.astype(jnp.float32) + update).astype(jnp.bfloat16)


def row_mask(tokens, rows, cols):
    def row_of(dim):
        at = lax.broadcasted_iota(jnp.int32, (tokens, tokens), dim)
        return lax.rem(lax.div(at, cols), rows)

    return row_of(0) == row_of(1)


def kernel(
    sizes,
    rows,
    cols,
    x_hbm,
    frame_gain_hbm,
    frame_qkv_hbm,
    frame_out_hbm,
    gain1_hbm,
    qkv1_hbm,
    out1_hbm,
    gain2_hbm,
    qkv2_hbm,
    out2_hbm,
    o_ref,
    x_ref,
    frame_gain_ref,
    frame_qkv_ref,
    frame_out_ref,
    gain1_ref,
    gain2_ref,
    parts,
    load_sem,
    whole,
    sent,
    got,
    mixed,
    returned,
    stream_ref,
    swapped,
    refined,
    back,
    part_sem,
    spread_send,
    spread_recv,
    hop_send,
    hop_recv,
    trio_send,
    trio_recv,
    mix_send,
    mix_recv,
    swap_send,
    swap_recv,
    back_send,
    back_recv,
):
    views, bands, batches = sizes["view"], sizes["band"], sizes["batch"]
    view, band, batch = lax.axis_index("view"), lax.axis_index("band"), lax.axis_index("batch")
    tokens = x_hbm.shape[0]
    inner = frame_out_hbm.shape[0]
    pair = inner // bands
    depth = qkv1_hbm.shape[0]
    share = parts.shape[2] // (views * batches)
    chunk = tokens // views

    hops = []
    for axis, at, size in (("view", view, views), ("batch", batch, batches)):
        step = size // 2
        while step:
            bit = lax.rem(lax.div(at, step), 2)
            hops.append((axis, at + step * (1 - 2 * bit), bit))
            step //= 2
    streams = [hops, hops[1::-1] + hops[2:]]
    half = depth // len(streams)
    indices = []
    for order in streams:
        index = 0
        for level, (_, _, bit) in enumerate(order):
            index = index + bit * 2**level
        indices.append(index)

    def ahead(d):
        return lax.rem(band + d, bands)

    def behind(d):
        return lax.rem(band + bands - d, bands)

    def other(d):
        return lax.rem(view + d, views)

    def remote(src, dst, send, recv, axis, to):
        return pltpu.make_async_remote_copy(
            src_ref=src,
            dst_ref=dst,
            send_sem=send,
            recv_sem=recv,
            device_id={axis: to},
            device_id_type=pl.DeviceIdType.MESH,
        )

    def share_at(layer, stream, k):
        at = pl.ds(pl.multiple_of(behind(k) * depth + stream * half, half), half)
        columns = pl.ds(pl.multiple_of(indices[stream] * share, share), share)
        return whole.at[layer, at, columns]

    def spread_own(layer, stream, toward):
        columns = pl.ds(pl.multiple_of(indices[stream] * share, share), share)
        return remote(
            parts.at[layer, stream * half : (stream + 1) * half, columns],
            share_at(layer, stream, 0),
            spread_send.at[layer, stream, 0 if toward == 1 else 1],
            spread_recv.at[layer, stream, 0 if toward == 1 else bands - 2],
            "band",
            band + toward,
        )

    def spread_on(layer, stream, k, toward):
        block = share_at(layer, stream, k)
        return remote(
            block,
            block,
            spread_send.at[layer, stream, 1 + k],
            spread_recv.at[layer, stream, k if toward == 1 else k - 2],
            "band",
            band + toward,
        )

    def spread_arrived(layer, stream, k):
        block = share_at(layer, stream, k)
        remote(
            block,
            block,
            spread_send.at[layer, stream, 0],
            spread_recv.at[layer, stream, k - 1],
            "band",
            ahead(1),
        ).wait_recv()

    def own_sends(layer, act):
        for stream in range(len(streams)):
            for toward, there in ((1, band < bands - 1), (-1, band > 0)):

                @pl.when(there)
                def _():
                    act(spread_own(layer, stream, toward))

    def forwards(layer, stream, k, act):
        @pl.when((k <= band) & (band < bands - 1))
        def _():
            act(spread_on(layer, stream, k, 1))

        @pl.when((k > band) & (band > 0))
        def _():
            act(spread_on(layer, stream, k, -1))

    def nearest(t):
        middle = (t + 1) // 2 if t % 2 else bands - t // 2
        return jnp.where(band == 0, bands - t, jnp.where(band == bands - 1, t, middle))

    def hop(layer, stream, level, k):
        axis, to, _ = streams[stream][level]
        held = share * 2**level
        at = pl.ds(pl.multiple_of(behind(k) * depth + stream * half, half), half)
        columns = pl.ds(
            pl.multiple_of(lax.div(indices[stream], 2**level) * held, held), held
        )
        block = whole.at[layer, at, columns]
        return remote(
            block,
            block,
            hop_send.at[layer, stream, level, k - 1],
            hop_recv.at[layer, stream, level, k - 1],
            axis,
            to,
        )

    def trio(d):
        return remote(
            sent.at[ahead(d)], got.at[band], trio_send.at[d - 1], trio_recv.at[d - 1], "band", ahead(d)
        )

    def mix(d):
        return remote(
            mixed.at[ahead(d)],
            returned.at[band],
            mix_send.at[d - 1],
            mix_recv.at[d - 1],
            "band",
            ahead(d),
        )

    def rows_of(at):
        return pl.ds(pl.multiple_of(at * chunk, chunk), chunk)

    def swap(src, dst, send, recv, d):
        return remote(
            src.at[rows_of(other(d))],
            dst.at[rows_of(view)],
            send.at[d - 1],
            recv.at[d - 1],
            "view",
            other(d),
        )

    def pass_on(layer, level):
        for t in range(1, bands):
            k = nearest(t)
            for stream in range(len(streams)):
                if level == 0:
                    spread_arrived(layer, stream, k)
                    forwards(layer, stream, k, lambda copy: copy.start())
                else:
                    hop(layer, stream, level - 1, k).wait_recv()
                if level < len(hops):
                    hop(layer, stream, level, k).start()

    loads = {}
    for at, (name, src, dst) in enumerate(
        (
            ("out1", out1_hbm, parts.at[0, :, 3 * inner :]),
            ("qkv1", qkv1_hbm, parts.at[0, :, : 3 * inner]),
            ("x", x_hbm, x_ref),
            ("frame_gain", frame_gain_hbm, frame_gain_ref),
            ("frame_qkv", frame_qkv_hbm, frame_qkv_ref),
            ("out2", out2_hbm, parts.at[1, :, 3 * inner :]),
            ("qkv2", qkv2_hbm, parts.at[1, :, : 3 * inner]),
            ("frame_out", frame_out_hbm, frame_out_ref),
            ("gain1", gain1_hbm, gain1_ref),
            ("gain2", gain2_hbm, gain2_ref),
        )
    ):
        loads[name] = pltpu.make_async_copy(src, dst, load_sem.at[at])

    barrier = pltpu.get_barrier_semaphore()
    greeted = 0
    for axis, at, size in (("band", band, bands), ("view", view, views)):
        for d in range(1, size):
            pl.semaphore_signal(
                barrier,
                inc=1,
                device_id={axis: lax.rem(at + d, size)},
                device_id_type=pl.DeviceIdType.MESH,
            )
            greeted += 1
    for axis, to, _ in hops:
        if axis == "batch":
            pl.semaphore_signal(
                barrier, inc=1, device_id={axis: to}, device_id_type=pl.DeviceIdType.MESH
            )
            greeted += 1
    own = pl.ds(pl.multiple_of(band * depth, depth), depth)
    for copy in loads.values():
        copy.start()
    own_parts = [
        pltpu.make_async_copy(parts.at[layer], whole.at[layer, own], part_sem.at[layer])
        for layer in range(2)
    ]

    loads["out1"].wait()
    loads["qkv1"].wait()
    pl.semaphore_wait(barrier, greeted)
    own_sends(0, lambda copy: copy.start())
    own_parts[0].start()
    loads["x"].wait()
    loads["frame_gain"].wait()
    normed = rms_normed(x_ref[...], frame_gain_ref[...])
    loads["frame_qkv"].wait()
    projected = jnp.dot(normed, frame_qkv_ref[...], preferred_element_type=jnp.float32)
    projected = projected.astype(jnp.bfloat16)
    for t in range(bands):
        for which in range(3):
            at = which * inner + t * pair
            sent[t, :, which * pair : (which + 1) * pair] = projected[:, at : at + pair]
    for d in range(1, bands):
        trio(d).start()
    loads["out2"].wait()
    loads["qkv2"].wait()
    own_parts[1].start()
    own_sends(1, lambda copy: copy.start())
    got[band] = sent[band]
    pass_on(0, 0)
    pass_on(0, 1)

    for d in range(1, bands):
        trio(d).wait_recv()
    everyone = got[...].reshape(bands * tokens, 3 * pair)

    def attend(at):
        queries = got[at]
        parts = []
        for lo in range(0, pair, 2 * HEAD_DIM):
            hi = lo + 2 * HEAD_DIM
            parts.append(
                attend_pair(
                    queries[:, lo:hi],
                    everyone[:, pair + lo : pair + hi],
                    everyone[:, 2 * pair + lo : 2 * pair + hi],
                    None,
                )
            )
        return jnp.concatenate(parts, axis=1) if len(parts) > 1 else parts[0]

    for d in range(1, bands):
        mixed[ahead(d)] = attend(ahead(d))
        mix(d).start()
    returned[band] = attend(band)
    pass_on(1, 0)
    for level in range(2, len(hops)):
        pass_on(0, level)
    for d in range(1, bands):
        mix(d).wait_recv()
    for name in ("frame_out", "gain1", "gain2"):
        loads[name].wait()
    attended = jnp.concatenate([returned[t] for t in range(bands)], axis=1)
    update = jnp.dot(attended, frame_out_ref[...], preferred_element_type=jnp.float32)
    stream_ref[...] = (x_ref[...].astype(jnp.float32) + update).astype(jnp.bfloat16)
    for d in range(1, views):
        swap(stream_ref, swapped, swap_send, swap_recv, d).start()
    swapped[rows_of(view)] = stream_ref[rows_of(view)]
    pass_on(1, 1)
    for d in range(1, views):
        swap(stream_ref, swapped, swap_send, swap_recv, d).wait_recv()
    for copy in own_parts:
        copy.wait()
    pass_on(0, len(hops))
    mask = row_mask(tokens, rows, cols)
    stream = row_layer(swapped[...], gain1_ref[...], whole.at[0], inner, mask)
    for level in range(2, len(hops) + 1):
        pass_on(1, level)
    refined[...] = row_layer(stream, gain2_ref[...], whole.at[1], inner, mask)
    for d in range(1, views):
        swap(refined, back, back_send, back_recv, d).start()
    back[rows_of(view)] = refined[rows_of(view)]
    for layer in range(2):
        own_sends(layer, lambda copy: copy.wait_send())
    for d in range(1, bands):
        for layer in range(2):
            for stream in range(len(streams)):
                forwards(layer, stream, d, lambda copy: copy.wait_send())
                for level in range(len(hops)):
                    hop(layer, stream, level, d).wait_send()
        trio(d).wait_send()
        mix(d).wait_send()
    for d in range(1, views):
        swap(stream_ref, swapped, swap_send, swap_recv, d).wait_send()
        swap(refined, back, back_send, back_recv, d).wait()
    o_ref[...] = back[...]


def local_swapped(
    sizes,
    images,
    frame_gain,
    frame_qkv,
    frame_out,
    row1_gain,
    row1_qkv,
    row1_out,
    row2_gain,
    row2_qkv,
    row2_out,
):
    _, row_count, col_count, width = images.shape
    inner = frame_out.shape[0]
    tokens = row_count * col_count
    views, bands, batches = sizes["view"], sizes["band"], sizes["batch"]
    depth = row1_qkv.shape[0]
    pair = inner // bands
    hops = (views * batches).bit_length() - 1
    vmem = pl.BlockSpec(memory_space=pltpu.VMEM)
    kind = jnp.bfloat16
    dma = pltpu.SemaphoreType.DMA
    refined = pl.pallas_call(
        functools.partial(kernel, sizes, row_count // views, col_count),
        out_shape=jax.ShapeDtypeStruct((tokens, width), kind),
        in_specs=[pl.BlockSpec(memory_space=pltpu.HBM)] * 10,
        out_specs=vmem,
        scratch_shapes=[
            pltpu.VMEM((tokens, width), kind),
            pltpu.VMEM(frame_gain.shape, frame_gain.dtype),
            pltpu.VMEM(frame_qkv.shape, kind),
            pltpu.VMEM(frame_out.shape, kind),
            pltpu.VMEM(row1_gain.shape, row1_gain.dtype),
            pltpu.VMEM(row2_gain.shape, row2_gain.dtype),
            pltpu.VMEM((2, depth, 4 * inner), kind),
            dma((10,)),
            pltpu.VMEM((2, bands * depth, 4 * inner), kind),
            pltpu.VMEM((bands, tokens, 3 * pair), kind),
            pltpu.VMEM((bands, tokens, 3 * pair), kind),
            pltpu.VMEM((bands, tokens, pair), kind),
            pltpu.VMEM((bands, tokens, pair), kind),
            pltpu.VMEM((tokens, width), kind),
            pltpu.VMEM((tokens, width), kind),
            pltpu.VMEM((tokens, width), kind),
            pltpu.VMEM((tokens, width), kind),
            dma((2,)),
            dma((2, 2, bands + 1)),
            dma((2, 2, bands - 1)),
            dma((2, 2, hops, bands - 1)),
            dma((2, 2, hops, bands - 1)),
            dma((bands - 1,)),
            dma((bands - 1,)),
            dma((bands - 1,)),
            dma((bands - 1,)),
            dma((views - 1,)),
            dma((views - 1,)),
            dma((views - 1,)),
            dma((views - 1,)),
        ],
        compiler_params=pltpu.CompilerParams(
            collective_id=0, has_side_effects=True, vmem_limit_bytes=63 * 1024 * 1024
        ),
    )(
        images.reshape(tokens, width),
        frame_gain,
        frame_qkv,
        frame_out,
        row1_gain,
        row1_qkv,
        row1_out.T,
        row2_gain,
        row2_qkv,
        row2_out.T,
    )
    return refined.reshape(images.shape)


def local(
    images,
    frame_gain,
    frame_qkv,
    frame_out,
    row1_gain,
    row1_qkv,
    row1_out,
    row2_gain,
    row2_qkv,
    row2_out,
):
    _, row_count, col_count, width = images.shape
    inner = frame_out.shape[0]
    heads = inner // HEAD_DIM
    tokens = row_count * col_count
    stream = images.reshape(tokens, width)
    normed = rms_normed(stream, frame_gain)
    start_state = (
        jnp.full((heads, tokens), -1e30, jnp.float32),
        jnp.zeros((heads, tokens), jnp.float32),
        jnp.zeros((tokens, heads, HEAD_DIM), jnp.float32),
    )
    queries = (
        jnp.dot(normed, frame_qkv[:, :inner], preferred_element_type=jnp.float32)
        .astype(jnp.bfloat16)
        .reshape(tokens, heads, HEAD_DIM)
    )
    piece = lax.all_gather(normed, "band", axis=0, tiled=True)
    count = piece.shape[0]
    paired = jnp.dot(piece, frame_qkv[:, inner:], preferred_element_type=jnp.float32).astype(
        jnp.bfloat16
    )
    result = online_update(
        start_state,
        queries,
        paired[:, :inner].reshape(count, heads, HEAD_DIM),
        paired[:, inner:].reshape(count, heads, HEAD_DIM),
    )
    _, total, accum = result
    attended = (
        (accum / jnp.transpose(total)[:, :, None]).astype(jnp.bfloat16).reshape(tokens, inner)
    )
    update = jnp.dot(attended, frame_out, preferred_element_type=jnp.float32)
    stream = (stream.astype(jnp.float32) + update).astype(jnp.bfloat16)
    stream = row_sublayer(
        stream,
        row_count,
        col_count,
        row1_gain,
        lambda normed_rows: project_parts(normed_rows, row1_qkv),
        lambda merged: mix_parts(merged, row1_out),
    )
    stream = row_sublayer(
        stream,
        row_count,
        col_count,
        row2_gain,
        lambda normed_rows: project_parts(normed_rows, row2_qkv),
        lambda merged: mix_parts(merged, row2_out),
    )
    return stream.reshape(images.shape)


def solution(mesh):
    in_specs = (
        P(("batch", "view"), "band", None, None),
        P(),
        P(),
        P(),
        P(),
        P("band", None),
        P(None, "band"),
        P(),
        P("band", None),
        P(None, "band"),
    )
    out_specs = P(("batch", "view"), "band", None, None)

    sizes = {name: mesh.shape[name] for name in ("view", "band", "batch")}

    def fits(images, frame_out, row_qkv):
        views, bands, batches = sizes["view"], sizes["band"], sizes["batch"]
        rows = images.shape[1] // bands
        inner, width = frame_out.shape
        depth = row_qkv.shape[0] // bands
        if min(views, bands, batches) < 2 or bands > 4 or rows % views:
            return False
        return (
            views & (views - 1) == 0
            and batches & (batches - 1) == 0
            and images.shape[0] == views * batches
            and rows * images.shape[2] // views % 16 == 0
            and depth % 32 == 0
            and width == row_qkv.shape[0]
            and inner % (bands * 2 * HEAD_DIM) == 0
            and 4 * inner % (128 * views * batches) == 0
        )

    def chosen(*arrays):
        fit = fits(arrays[0], arrays[3], arrays[5])
        body = functools.partial(local_swapped, sizes) if fit else local
        return jax.shard_map(
            body, mesh=mesh, in_specs=in_specs, out_specs=out_specs, check_vma=False
        )(*arrays)

    return chosen
```

```python
import functools

import jax
import jax.numpy as jnp
from jax import lax
from jax.experimental import pallas as pl
from jax.experimental.pallas import tpu as pltpu
from jax.sharding import PartitionSpec as P

HEAD_DIM = 64


EPSILON = 1e-06
BLOCK_ROWS = 512


def rms_normed(stream, gain):
    values = stream.astype(jnp.float32)
    factor = lax.rsqrt(jnp.mean(values * values, axis=-1, keepdims=True) + EPSILON)
    return (values * factor * gain).astype(jnp.bfloat16)


def online_update(carry, queries, keys, values):
    running, total, accum = carry
    scores = jnp.einsum(
        "qhd,khd->hqk", queries, keys, preferred_element_type=jnp.float32
    ) * HEAD_DIM ** (-0.5)
    highest = jnp.maximum(running, jnp.max(scores, axis=-1))
    weights = jnp.exp(scores - highest[:, :, None])
    total = jnp.sum(weights, axis=-1)
    mixed = jnp.einsum(
        "hqk,khd->qhd", weights.astype(jnp.bfloat16), values, preferred_element_type=jnp.float32
    )
    accum = mixed
    return (highest, total, accum)


def unit_attention(trio):
    queries, keys, values = trio
    length, pair_width = queries.shape
    block = min(BLOCK_ROWS, length)
    keys = keys.reshape(length, 2, HEAD_DIM)
    values = values.reshape(length, 2, HEAD_DIM)
    blocks = queries.reshape(length // block, block, 2, HEAD_DIM)

    def one_block(query_block):
        scores = jnp.einsum(
            "qhd,khd->hqk", query_block, keys, preferred_element_type=jnp.float32
        ) * HEAD_DIM ** (-0.5)
        weights = jnp.exp(scores - jnp.max(scores, axis=-1, keepdims=True))
        mixed = jnp.einsum(
            "hqk,khd->qhd", weights.astype(jnp.bfloat16), values, preferred_element_type=jnp.float32
        )
        total = jnp.transpose(jnp.sum(weights, axis=-1))
        return (mixed / total[:, :, None]).astype(jnp.bfloat16).reshape(block, pair_width)

    return lax.map(one_block, blocks).reshape(length, pair_width)


def attend_units(pieces):
    queries, keys, values = pieces
    attended = lax.map(unit_attention, (queries[0], keys[0], values[0]))
    return lax.all_to_all(attended[None], "view", split_axis=2, concat_axis=0, tiled=True)


def project_parts(normed, shard):
    groups = shard.shape[1] // (2 * HEAD_DIM)
    piece = lax.all_gather(shard, "band", axis=0, tiled=True)
    count = piece.shape[0]
    return jnp.einsum(
        "rcd,dpw->rpcw",
        normed,
        piece.reshape(count, groups, 2 * HEAD_DIM),
        preferred_element_type=jnp.float32,
    )


def mix_parts(merged, shard):
    groups = merged.shape[1]
    piece = lax.all_gather(shard, "band", axis=1, tiled=True)
    count = piece.shape[1]
    return jnp.einsum(
        "rpcw,pwn->rcn",
        merged,
        piece.reshape(groups, 2 * HEAD_DIM, count),
        preferred_element_type=jnp.float32,
    )


def row_sublayer(stream, row_count, col_count, gain, project, mix):
    width = stream.shape[1]
    normed = rms_normed(stream, gain).reshape(row_count, col_count, width)
    projected = project(normed)
    groups = projected.shape[1] // 3
    views = lax.axis_size("view")

    def unit_layout(section):
        return section.astype(jnp.bfloat16).reshape(
            views, row_count * groups // views, col_count, 2 * HEAD_DIM
        )

    triple = (
        unit_layout(projected[:, :groups]),
        unit_layout(projected[:, groups : 2 * groups]),
        unit_layout(projected[:, 2 * groups :]),
    )
    returned = attend_units(
        (
            lax.all_to_all(triple[0], "view", split_axis=0, concat_axis=2, tiled=True),
            lax.all_to_all(triple[1], "view", split_axis=0, concat_axis=2, tiled=True),
            lax.all_to_all(triple[2], "view", split_axis=0, concat_axis=2, tiled=True),
        )
    )
    merged = returned.reshape(row_count, groups, col_count, 2 * HEAD_DIM)
    update = mix(merged).reshape(row_count * col_count, width)
    return (stream.astype(jnp.float32) + update).astype(jnp.bfloat16)


def attend_pair(queries, keys, values, mask):
    lane = lax.broadcasted_iota(jnp.int32, queries.shape, 1)
    sides = []
    for side in range(2):
        own = (lane >= side * HEAD_DIM) & (lane < (side + 1) * HEAD_DIM)
        scores = lax.dot_general(
            jnp.where(own, queries, jnp.zeros_like(queries)),
            keys,
            (((1,), (1,)), ((), ())),
            preferred_element_type=jnp.float32,
        ) * HEAD_DIM ** (-0.5)
        if mask is not None:
            scores = jnp.where(mask, scores, -jnp.inf)
        weights = jnp.exp(scores - jnp.max(scores, axis=-1, keepdims=True))
        total = jnp.sum(weights, axis=-1, keepdims=True)
        mixed = jnp.dot(weights.astype(jnp.bfloat16), values, preferred_element_type=jnp.float32)
        sides.append(mixed / total)
    return jnp.where(lane < HEAD_DIM, sides[0], sides[1]).astype(jnp.bfloat16)


def row_layer(stream, gain, weights, inner, mask):
    pair = 2 * HEAD_DIM
    normed = rms_normed(stream, gain)
    projected = jnp.dot(normed, weights[:, : 3 * inner], preferred_element_type=jnp.float32)
    projected = projected.astype(jnp.bfloat16)
    parts = []
    for at in range(0, inner, pair):
        parts.append(
            attend_pair(
                projected[:, at : at + pair],
                projected[:, inner + at : inner + at + pair],
                projected[:, 2 * inner + at : 2 * inner + at + pair],
                mask,
            )
        )
    attended = jnp.concatenate(parts, axis=1)
    update = lax.dot_general(
        attended,
        weights[:, 3 * inner :],
        (((1,), (1,)), ((), ())),
        preferred_element_type=jnp.float32,
    )
    return (stream.astype(jnp.float32) + update).astype(jnp.bfloat16)


def row_mask(tokens, rows, cols):
    def row_of(dim):
        at = lax.broadcasted_iota(jnp.int32, (tokens, tokens), dim)
        return lax.rem(lax.div(at, cols), rows)

    return row_of(0) == row_of(1)


def kernel(
    sizes,
    rows,
    cols,
    x_hbm,
    frame_gain_hbm,
    frame_qkv_hbm,
    frame_out_hbm,
    gain1_hbm,
    qkv1_hbm,
    out1_hbm,
    gain2_hbm,
    qkv2_hbm,
    out2_hbm,
    o_ref,
    x_ref,
    frame_gain_ref,
    frame_qkv_ref,
    frame_out_ref,
    gain1_ref,
    gain2_ref,
    parts,
    load_sem,
    whole,
    sent,
    got,
    mixed,
    returned,
    stream_ref,
    swapped,
    refined,
    back,
    part_sem,
    spread_send,
    spread_recv,
    hop_send,
    hop_recv,
    trio_send,
    trio_recv,
    mix_send,
    mix_recv,
    swap_send,
    swap_recv,
    back_send,
    back_recv,
):
    views, bands, batches = sizes["view"], sizes["band"], sizes["batch"]
    view, band, batch = lax.axis_index("view"), lax.axis_index("band"), lax.axis_index("batch")
    tokens = x_hbm.shape[0]
    inner = frame_out_hbm.shape[0]
    pair = inner // bands
    depth = qkv1_hbm.shape[0]
    share = parts.shape[2] // (views * batches)
    chunk = tokens // views

    hops = []
    for axis, at, size in (("view", view, views), ("batch", batch, batches)):
        step = size // 2
        while step:
            bit = lax.rem(lax.div(at, step), 2)
            hops.append((axis, at + step * (1 - 2 * bit), bit))
            step //= 2
    streams = [hops, hops[1::-1] + hops[2:]]
    half = depth // len(streams)
    indices = []
    for order in streams:
        index = 0
        for level, (_, _, bit) in enumerate(order):
            index = index + bit * 2**level
        indices.append(index)

    def ahead(d):
        return lax.rem(band + d, bands)

    def behind(d):
        return lax.rem(band + bands - d, bands)

    def other(d):
        return lax.rem(view + d, views)

    def remote(src, dst, send, recv, axis, to):
        return pltpu.make_async_remote_copy(
            src_ref=src,
            dst_ref=dst,
            send_sem=send,
            recv_sem=recv,
            device_id={axis: to},
            device_id_type=pl.DeviceIdType.MESH,
        )

    def share_at(layer, stream, k):
        at = pl.ds(pl.multiple_of(behind(k) * depth + stream * half, half), half)
        columns = pl.ds(pl.multiple_of(indices[stream] * share, share), share)
        return whole.at[layer, at, columns]

    def spread_own(layer, stream, toward):
        columns = pl.ds(pl.multiple_of(indices[stream] * share, share), share)
        return remote(
            parts.at[layer, stream * half : (stream + 1) * half, columns],
            share_at(layer, stream, 0),
            spread_send.at[layer, stream, 0 if toward == 1 else 1],
            spread_recv.at[layer, stream, 0 if toward == 1 else bands - 2],
            "band",
            band + toward,
        )

    def spread_on(layer, stream, k, toward):
        block = share_at(layer, stream, k)
        return remote(
            block,
            block,
            spread_send.at[layer, stream, 1 + k],
            spread_recv.at[layer, stream, k if toward == 1 else k - 2],
            "band",
            band + toward,
        )

    def spread_arrived(layer, stream, k):
        block = share_at(layer, stream, k)
        remote(
            block,
            block,
            spread_send.at[layer, stream, 0],
            spread_recv.at[layer, stream, k - 1],
            "band",
            ahead(1),
        ).wait_recv()

    def own_sends(layer, act):
        for stream in range(len(streams)):
            for toward, there in ((1, band < bands - 1), (-1, band > 0)):

                @pl.when(there)
                def _():
                    act(spread_own(layer, stream, toward))

    def forwards(layer, stream, k, act):
        @pl.when((k <= band) & (band < bands - 1))
        def _():
            act(spread_on(layer, stream, k, 1))

        @pl.when((k > band) & (band > 0))
        def _():
            act(spread_on(layer, stream, k, -1))

    def nearest(t):
        middle = (t + 1) // 2 if t % 2 else bands - t // 2
        return jnp.where(band == 0, bands - t, jnp.where(band == bands - 1, t, middle))

    def hop(layer, stream, level, k):
        axis, to, _ = streams[stream][level]
        held = share * 2**level
        at = pl.ds(pl.multiple_of(behind(k) * depth + stream * half, half), half)
        columns = pl.ds(
            pl.multiple_of(lax.div(indices[stream], 2**level) * held, held), held
        )
        block = whole.at[layer, at, columns]
        return remote(
            block,
            block,
            hop_send.at[layer, stream, level, k - 1],
            hop_recv.at[layer, stream, level, k - 1],
            axis,
            to,
        )

    def trio(d):
        return remote(
            sent.at[ahead(d)], got.at[band], trio_send.at[d - 1], trio_recv.at[d - 1], "band", ahead(d)
        )

    def mix(d):
        return remote(
            mixed.at[ahead(d)],
            returned.at[band],
            mix_send.at[d - 1],
            mix_recv.at[d - 1],
            "band",
            ahead(d),
        )

    def rows_of(at):
        return pl.ds(pl.multiple_of(at * chunk, chunk), chunk)

    def swap(src, dst, send, recv, d):
        return remote(
            src.at[rows_of(other(d))],
            dst.at[rows_of(view)],
            send.at[d - 1],
            recv.at[d - 1],
            "view",
            other(d),
        )

    def pass_on(layer, level, turns=range(1, bands)):
        for t in turns:
            k = nearest(t)
            for stream in range(len(streams)):
                if level == 0:
                    spread_arrived(layer, stream, k)
                    forwards(layer, stream, k, lambda copy: copy.start())
                else:
                    hop(layer, stream, level - 1, k).wait_recv()
                if level < len(hops):
                    hop(layer, stream, level, k).start()

    loads = {}
    for at, (name, src, dst) in enumerate(
        (
            ("out1", out1_hbm, parts.at[0, :, 3 * inner :]),
            ("qkv1", qkv1_hbm, parts.at[0, :, : 3 * inner]),
            ("x", x_hbm, x_ref),
            ("frame_gain", frame_gain_hbm, frame_gain_ref),
            ("frame_qkv", frame_qkv_hbm, frame_qkv_ref),
            ("out2", out2_hbm, parts.at[1, :, 3 * inner :]),
            ("qkv2", qkv2_hbm, parts.at[1, :, : 3 * inner]),
            ("frame_out", frame_out_hbm, frame_out_ref),
            ("gain1", gain1_hbm, gain1_ref),
            ("gain2", gain2_hbm, gain2_ref),
        )
    ):
        loads[name] = pltpu.make_async_copy(src, dst, load_sem.at[at])

    barrier = pltpu.get_barrier_semaphore()
    greeted = 0
    for axis, at, size in (("band", band, bands), ("view", view, views)):
        for d in range(1, size):
            pl.semaphore_signal(
                barrier,
                inc=1,
                device_id={axis: lax.rem(at + d, size)},
                device_id_type=pl.DeviceIdType.MESH,
            )
            greeted += 1
    for axis, to, _ in hops:
        if axis == "batch":
            pl.semaphore_signal(
                barrier, inc=1, device_id={axis: to}, device_id_type=pl.DeviceIdType.MESH
            )
            greeted += 1
    own = pl.ds(pl.multiple_of(band * depth, depth), depth)
    for copy in loads.values():
        copy.start()
    own_parts = [
        pltpu.make_async_copy(parts.at[layer], whole.at[layer, own], part_sem.at[layer])
        for layer in range(2)
    ]

    loads["out1"].wait()
    loads["qkv1"].wait()
    pl.semaphore_wait(barrier, greeted)
    own_sends(0, lambda copy: copy.start())
    own_parts[0].start()
    loads["x"].wait()
    loads["frame_gain"].wait()
    normed = rms_normed(x_ref[...], frame_gain_ref[...])
    loads["frame_qkv"].wait()
    projected = jnp.dot(normed, frame_qkv_ref[...], preferred_element_type=jnp.float32)
    projected = projected.astype(jnp.bfloat16)
    for t in range(bands):
        for which in range(3):
            at = which * inner + t * pair
            sent[t, :, which * pair : (which + 1) * pair] = projected[:, at : at + pair]
    for d in range(1, bands):
        trio(d).start()
    loads["out2"].wait()
    loads["qkv2"].wait()
    own_parts[1].start()
    own_sends(1, lambda copy: copy.start())
    got[band] = sent[band]
    pass_on(0, 0)
    pass_on(0, 1)

    for d in range(1, bands):
        trio(d).wait_recv()
    everyone = got[...].reshape(bands * tokens, 3 * pair)

    def attend(at):
        queries = got[at]
        parts = []
        for lo in range(0, pair, 2 * HEAD_DIM):
            hi = lo + 2 * HEAD_DIM
            parts.append(
                attend_pair(
                    queries[:, lo:hi],
                    everyone[:, pair + lo : pair + hi],
                    everyone[:, 2 * pair + lo : 2 * pair + hi],
                    None,
                )
            )
        return jnp.concatenate(parts, axis=1) if len(parts) > 1 else parts[0]

    for d in range(1, bands):
        mixed[ahead(d)] = attend(ahead(d))
        mix(d).start()
        pass_on(1, 0, (d,))
    returned[band] = attend(band)
    for level in range(2, len(hops)):
        pass_on(0, level)
    for d in range(1, bands):
        mix(d).wait_recv()
    for name in ("frame_out", "gain1", "gain2"):
        loads[name].wait()
    attended = jnp.concatenate([returned[t] for t in range(bands)], axis=1)
    update = jnp.dot(attended, frame_out_ref[...], preferred_element_type=jnp.float32)
    stream_ref[...] = (x_ref[...].astype(jnp.float32) + update).astype(jnp.bfloat16)
    for d in range(1, views):
        swap(stream_ref, swapped, swap_send, swap_recv, d).start()
    swapped[rows_of(view)] = stream_ref[rows_of(view)]
    pass_on(1, 1)
    for d in range(1, views):
        swap(stream_ref, swapped, swap_send, swap_recv, d).wait_recv()
    for copy in own_parts:
        copy.wait()
    pass_on(0, len(hops))
    mask = row_mask(tokens, rows, cols)
    stream = row_layer(swapped[...], gain1_ref[...], whole.at[0], inner, mask)
    for level in range(2, len(hops) + 1):
        pass_on(1, level)
    refined[...] = row_layer(stream, gain2_ref[...], whole.at[1], inner, mask)
    for d in range(1, views):
        swap(refined, back, back_send, back_recv, d).start()
    back[rows_of(view)] = refined[rows_of(view)]
    for layer in range(2):
        own_sends(layer, lambda copy: copy.wait_send())
    for d in range(1, bands):
        for layer in range(2):
            for stream in range(len(streams)):
                forwards(layer, stream, d, lambda copy: copy.wait_send())
                for level in range(len(hops)):
                    hop(layer, stream, level, d).wait_send()
        trio(d).wait_send()
        mix(d).wait_send()
    for d in range(1, views):
        swap(stream_ref, swapped, swap_send, swap_recv, d).wait_send()
        swap(refined, back, back_send, back_recv, d).wait()
    o_ref[...] = back[...]


def local_swapped(
    sizes,
    images,
    frame_gain,
    frame_qkv,
    frame_out,
    row1_gain,
    row1_qkv,
    row1_out,
    row2_gain,
    row2_qkv,
    row2_out,
):
    _, row_count, col_count, width = images.shape
    inner = frame_out.shape[0]
    tokens = row_count * col_count
    views, bands, batches = sizes["view"], sizes["band"], sizes["batch"]
    depth = row1_qkv.shape[0]
    pair = inner // bands
    hops = (views * batches).bit_length() - 1
    vmem = pl.BlockSpec(memory_space=pltpu.VMEM)
    kind = jnp.bfloat16
    dma = pltpu.SemaphoreType.DMA
    refined = pl.pallas_call(
        functools.partial(kernel, sizes, row_count // views, col_count),
        out_shape=jax.ShapeDtypeStruct((tokens, width), kind),
        in_specs=[pl.BlockSpec(memory_space=pltpu.HBM)] * 10,
        out_specs=vmem,
        scratch_shapes=[
            pltpu.VMEM((tokens, width), kind),
            pltpu.VMEM(frame_gain.shape, frame_gain.dtype),
            pltpu.VMEM(frame_qkv.shape, kind),
            pltpu.VMEM(frame_out.shape, kind),
            pltpu.VMEM(row1_gain.shape, row1_gain.dtype),
            pltpu.VMEM(row2_gain.shape, row2_gain.dtype),
            pltpu.VMEM((2, depth, 4 * inner), kind),
            dma((10,)),
            pltpu.VMEM((2, bands * depth, 4 * inner), kind),
            pltpu.VMEM((bands, tokens, 3 * pair), kind),
            pltpu.VMEM((bands, tokens, 3 * pair), kind),
            pltpu.VMEM((bands, tokens, pair), kind),
            pltpu.VMEM((bands, tokens, pair), kind),
            pltpu.VMEM((tokens, width), kind),
            pltpu.VMEM((tokens, width), kind),
            pltpu.VMEM((tokens, width), kind),
            pltpu.VMEM((tokens, width), kind),
            dma((2,)),
            dma((2, 2, bands + 1)),
            dma((2, 2, bands - 1)),
            dma((2, 2, hops, bands - 1)),
            dma((2, 2, hops, bands - 1)),
            dma((bands - 1,)),
            dma((bands - 1,)),
            dma((bands - 1,)),
            dma((bands - 1,)),
            dma((views - 1,)),
            dma((views - 1,)),
            dma((views - 1,)),
            dma((views - 1,)),
        ],
        compiler_params=pltpu.CompilerParams(
            collective_id=0, has_side_effects=True, vmem_limit_bytes=63 * 1024 * 1024
        ),
    )(
        images.reshape(tokens, width),
        frame_gain,
        frame_qkv,
        frame_out,
        row1_gain,
        row1_qkv,
        row1_out.T,
        row2_gain,
        row2_qkv,
        row2_out.T,
    )
    return refined.reshape(images.shape)


def local(
    images,
    frame_gain,
    frame_qkv,
    frame_out,
    row1_gain,
    row1_qkv,
    row1_out,
    row2_gain,
    row2_qkv,
    row2_out,
):
    _, row_count, col_count, width = images.shape
    inner = frame_out.shape[0]
    heads = inner // HEAD_DIM
    tokens = row_count * col_count
    stream = images.reshape(tokens, width)
    normed = rms_normed(stream, frame_gain)
    start_state = (
        jnp.full((heads, tokens), -1e30, jnp.float32),
        jnp.zeros((heads, tokens), jnp.float32),
        jnp.zeros((tokens, heads, HEAD_DIM), jnp.float32),
    )
    queries = (
        jnp.dot(normed, frame_qkv[:, :inner], preferred_element_type=jnp.float32)
        .astype(jnp.bfloat16)
        .reshape(tokens, heads, HEAD_DIM)
    )
    piece = lax.all_gather(normed, "band", axis=0, tiled=True)
    count = piece.shape[0]
    paired = jnp.dot(piece, frame_qkv[:, inner:], preferred_element_type=jnp.float32).astype(
        jnp.bfloat16
    )
    result = online_update(
        start_state,
        queries,
        paired[:, :inner].reshape(count, heads, HEAD_DIM),
        paired[:, inner:].reshape(count, heads, HEAD_DIM),
    )
    _, total, accum = result
    attended = (
        (accum / jnp.transpose(total)[:, :, None]).astype(jnp.bfloat16).reshape(tokens, inner)
    )
    update = jnp.dot(attended, frame_out, preferred_element_type=jnp.float32)
    stream = (stream.astype(jnp.float32) + update).astype(jnp.bfloat16)
    stream = row_sublayer(
        stream,
        row_count,
        col_count,
        row1_gain,
        lambda normed_rows: project_parts(normed_rows, row1_qkv),
        lambda merged: mix_parts(merged, row1_out),
    )
    stream = row_sublayer(
        stream,
        row_count,
        col_count,
        row2_gain,
        lambda normed_rows: project_parts(normed_rows, row2_qkv),
        lambda merged: mix_parts(merged, row2_out),
    )
    return stream.reshape(images.shape)


def solution(mesh):
    in_specs = (
        P(("batch", "view"), "band", None, None),
        P(),
        P(),
        P(),
        P(),
        P("band", None),
        P(None, "band"),
        P(),
        P("band", None),
        P(None, "band"),
    )
    out_specs = P(("batch", "view"), "band", None, None)

    sizes = {name: mesh.shape[name] for name in ("view", "band", "batch")}

    def fits(images, frame_out, row_qkv):
        views, bands, batches = sizes["view"], sizes["band"], sizes["batch"]
        rows = images.shape[1] // bands
        inner, width = frame_out.shape
        depth = row_qkv.shape[0] // bands
        if min(views, bands, batches) < 2 or bands > 4 or rows % views:
            return False
        return (
            views & (views - 1) == 0
            and batches & (batches - 1) == 0
            and images.shape[0] == views * batches
            and rows * images.shape[2] // views % 16 == 0
            and depth % 32 == 0
            and width == row_qkv.shape[0]
            and inner % (bands * 2 * HEAD_DIM) == 0
            and 4 * inner % (128 * views * batches) == 0
        )

    def chosen(*arrays):
        fit = fits(arrays[0], arrays[3], arrays[5])
        body = functools.partial(local_swapped, sizes) if fit else local
        return jax.shard_map(
            body, mesh=mesh, in_specs=in_specs, out_specs=out_specs, check_vma=False
        )(*arrays)

    return chosen
```
